32 devices in a mesh: groups: 2 (over x), tm: 8 (over z, y), chan: 2 (over core).
Axes of the slice: x: 2, y: 2, z: 4, core: 2. Of those that a mesh axis runs over, the one named last changes fastest.
Arguments:
- signal: bfloat16 [65536, 256], P(('groups', 'tm'), 'chan'), parts along dimension 0, may hold values from -6 to 6
- cotangent: bfloat16 [65536, 256], P(('groups', 'tm'), 'chan'), parts along dimension 0, may hold values from -6 to 6
- conv_weight: bfloat16 [2, 2, 256, 2, 256], replicated, may hold values from -0.25 to 0.25
- out_weight: bfloat16 [2, 256, 256], replicated, may hold values from -0.375 to 0.375
Outputs:
- output: bfloat16 [65536, 256], P(('groups', 'tm'), 'chan'), parts along dimension 0
- in_grad: bfloat16 [65536, 256], P(('groups', 'tm'), 'chan'), parts along dimension 0
- conv_grad: float32 [4, 2, 256, 2, 256], P('groups', None, None, None, 'chan'), parts along dimension 0
- out_grad: float32 [4, 256, 256], P('groups', None, 'chan'), parts along dimension 0
The draws below stay inside these ranges and needn't reach their ends.
There are 2 independent parts, one for each index of `groups`. The reference program is written for one: setup_inputs(seed, part) draws one part's arguments, and reference() takes and returns one part's arrays. A program takes and returns all parts, laid end to end along the dimension named above; an argument that names none is the same for every part. Nothing has to cross between parts.
All inputs are finite; a program needn't handle non-finite values.
Results may differ from the reference program's by a relative error of at most 0.0058.
Values may be sent and summed in bfloat16 or wider, within the bound.
No kernel may reach another device: no remote copies, remote signals or barrier semaphores. Data moves between devices by JAX's collectives and lax.ppermute only.
A program may use at most 128 MiB of HBM per device.

```python
import math
import jax
import jax.numpy as jnp

CH = 256
NL = 2
FIRST_DILATION = 2048
SECOND_DILATION = 8192
SAMPLES = 32768


def steps_of(key, shape, cuts, smallest, largest):
    level, own = 1.0, jax.random.fold_in(key, 6)
    for position, shards_of in cuts:
        steps = jnp.exp(jax.random.uniform(jax.random.fold_in(own, position), (shards_of,), jnp.float32, smallest / len(cuts), largest / len(cuts)))
        level = level * jnp.repeat(steps, shape[position] // shards_of).reshape([-1 if axis == position else 1 for axis in range(len(shape))])
    return level


def centred(rng, shape, scale, bound, pieces=(), kind=jnp.bfloat16):
    level = steps_of(rng, shape, pieces, -0.22, 0.18) if pieces else 1.0
    drawn = jax.random.normal(rng, shape, jnp.float32) * scale * level
    return jnp.minimum(jnp.maximum(drawn, -bound), bound).astype(kind)


def setup_inputs(seed: int = 0, part: int = 0) -> dict:
    seeds = jax.random.split(jax.random.key(seed), 5)
    part_splits = jax.random.split(jax.random.fold_in(seeds[4], part), 5)
    signal = centred(part_splits[0], (SAMPLES, CH), 1.0, 6.0, ((0, 8), (1, 2)))
    cotangent = centred(part_splits[1], (SAMPLES, CH), 1.0, 6.0, ((0, 8), (1, 2)))
    conv_weight = centred(seeds[2], (NL, 2, CH, 2, CH), (2 * CH) ** -0.5, 0.25)
    out_weight = centred(seeds[3], (NL, CH, CH), CH ** -0.5, 0.375)
    return {"signal": signal, "cotangent": cotangent, "conv_weight": conv_weight, "out_weight": out_weight}


def delay_rows(values, delay_span):
    padding = jnp.zeros((delay_span, values.shape[1]), values.dtype)
    return jnp.concatenate([padding, values[:values.shape[0] - delay_span]], axis=0)

def forward_shift_rows(values, delay_span):
    padding = jnp.zeros((delay_span, values.shape[1]), values.dtype)
    return jnp.concatenate([values[delay_span:], padding], axis=0)

def reference(signal, cotangent, conv_weight, out_weight):
    dilation_list = (FIRST_DILATION, SECOND_DILATION)
    scale_factor = 1.0 / math.sqrt(SAMPLES)
    present_signal = signal
    stored = []
    for layer_index in range(NL):
        delay_span = dilation_list[layer_index]
        delayed = delay_rows(present_signal, delay_span)
        tap_now = conv_weight[layer_index, 0].reshape(CH, 2 * CH)
        tap_past = conv_weight[layer_index, 1].reshape(CH, 2 * CH)
        preact = jnp.dot(present_signal, tap_now, preferred_element_type=jnp.float32) + jnp.dot(delayed, tap_past, preferred_element_type=jnp.float32)
        preact = preact.reshape(-1, 2, CH)
        filter_act = jnp.tanh(preact[:, 0, :])
        gate_act = jax.nn.sigmoid(preact[:, 1, :])
        hidden = (filter_act * gate_act).astype(jnp.bfloat16)
        following = (present_signal.astype(jnp.float32) + jnp.dot(hidden, out_weight[layer_index], preferred_element_type=jnp.float32)).astype(jnp.bfloat16)
        stored.append((present_signal, delayed, filter_act, gate_act, hidden))
        present_signal = following
    output = present_signal
    upstream = cotangent
    conv_list = [None] * NL
    out_list = [None] * NL
    for layer_index in reversed(range(NL)):
        delay_span = dilation_list[layer_index]
        layer_input, delayed, filter_act, gate_act, hidden = stored[layer_index]
        tap_now = conv_weight[layer_index, 0].reshape(CH, 2 * CH)
        tap_past = conv_weight[layer_index, 1].reshape(CH, 2 * CH)
        hidden_grad = jnp.dot(upstream, out_weight[layer_index].T, preferred_element_type=jnp.float32)
        filter_grad = hidden_grad * gate_act * (1.0 - filter_act * filter_act)
        gate_grad = hidden_grad * filter_act * gate_act * (1.0 - gate_act)
        pre_grad = jnp.stack([filter_grad, gate_grad], axis=1).astype(jnp.bfloat16).reshape(-1, 2 * CH)
        ahead_grad = forward_shift_rows(pre_grad, delay_span)
        out_list[layer_index] = jnp.dot(hidden.T, upstream, preferred_element_type=jnp.float32) * scale_factor
        conv_now = jnp.dot(layer_input.T, pre_grad, preferred_element_type=jnp.float32)
        conv_past = jnp.dot(delayed.T, pre_grad, preferred_element_type=jnp.float32)
        conv_list[layer_index] = jnp.stack([conv_now, conv_past]).reshape(2, CH, 2, CH) * scale_factor
        summed = jnp.dot(pre_grad, tap_now.T, preferred_element_type=jnp.float32) + jnp.dot(ahead_grad, tap_past.T, preferred_element_type=jnp.float32)
        upstream = (upstream.astype(jnp.float32) + summed).astype(jnp.bfloat16)
    return (output, upstream, jnp.stack(conv_list), jnp.stack(out_list))
```

```python
import functools
import math

import jax
import jax.numpy as jnp
from jax import lax
from jax.experimental import pallas as pl
from jax.experimental.pallas import tpu as pltpu
from jax.sharding import PartitionSpec as P

BF = jnp.bfloat16
F32 = jnp.float32
VMEM_LIMIT = 48 * 1024 * 1024


def mm(a, b):
    return jnp.dot(a, b, preferred_element_type=F32)


def mm_t(a, b):
    return lax.dot_general(a, b, (((1,), (1,)), ((), ())), preferred_element_type=F32)


def mm_rows(a, b):
    return lax.dot_general(a, b, (((0,), (0,)), ((), ())), preferred_element_type=F32)


def ordered(core, own, other):
    first = core == 0
    return jnp.concatenate(
        [jnp.where(first, own, other), jnp.where(first, other, own)], axis=1
    )


def halves(core, values):
    width = values.shape[1] // 2
    low, high = values[:, :width], values[:, width:]
    first = core == 0
    return jnp.where(first, low, high), jnp.where(first, high, low)


def gated(x, delayed, tap_now, tap_past):
    width = x.shape[1]
    preact = mm(x, tap_now) + mm(delayed, tap_past)
    filt = jnp.tanh(preact[:, :width])
    gate = 0.5 * jnp.tanh(0.5 * preact[:, width:]) + 0.5
    hidden = (filt * gate).astype(BF)
    slope_f = gate * (1.0 - filt * filt)
    slope_g = filt * gate * (1.0 - gate)
    return hidden, slope_f, slope_g


def call(body, scalars, grid, ins, outs, scratch=(), flops=0, moved=0):
    return pl.pallas_call(
        body,
        grid_spec=pltpu.PrefetchScalarGridSpec(
            num_scalar_prefetch=1,
            grid=grid,
            in_specs=[pl.BlockSpec(block, index) for _, block, index in ins],
            out_specs=[pl.BlockSpec(block, index) for _, _, block, index in outs],
            scratch_shapes=list(scratch),
        ),
        out_shape=[jax.ShapeDtypeStruct(shape, kind) for shape, kind, _, _ in outs],
        compiler_params=pltpu.CompilerParams(vmem_limit_bytes=VMEM_LIMIT),
        cost_estimate=pl.CostEstimate(flops=flops, bytes_accessed=moved, transcendentals=0),
    )(scalars, *[array for array, _, _ in ins])


def rows_map(i, s):
    return (i, 0)


def fixed_map(i, s):
    return (0, 0)


def whole(array):
    return (array, array.shape, fixed_map)


def by_rows(array, block):
    return (array, (block, array.shape[1]), rows_map)


def out_rows(rows, cols, kind, block):
    return ((rows, cols), kind, (block, cols), rows_map)


def first_b(ids, own, other, own_a, other_a, t0, t1, wo, x_o, xa_o, x1_o, hid_o, slope_o):
    core = ids[0]
    x = ordered(core, own[...], other[...])
    delayed = ordered(core, own_a[...], other_a[...])
    x_o[...] = x
    xa_o[...] = delayed
    hidden, sf, sg = gated(x, delayed, t0[...], t1[...])
    x1_o[...] = (x.astype(F32) + mm(hidden, wo[...])).astype(BF)
    hid_o[...] = hidden
    width = x.shape[1]
    slope_o[:, :width] = sf
    slope_o[:, width:] = sg


def first_a(ids, x_r, own_h, other_h, t0, t1, wo, xh_o, x1_o, hid_o, slope_o):
    core = ids[0]
    x = x_r[...]
    delayed = ordered(core, own_h[...], other_h[...])
    xh_o[...] = delayed
    hidden, sf, sg = gated(x, delayed, t0[...], t1[...])
    x1_o[...] = (x.astype(F32) + mm(hidden, wo[...])).astype(BF)
    hid_o[...] = hidden
    width = x.shape[1]
    slope_o[:, :width] = sf
    slope_o[:, width:] = sg


def cot_body(ids, own, other, wo, g_o, hg_o):
    g = ordered(ids[0], own[...], other[...])
    g_o[...] = g
    hg_o[...] = mm_t(g, wo[...])


def second(ids, x_r, d_r, hg_r, t0, t1, pre_o, past_o, hid_o):
    hidden, sf, sg = gated(x_r[...], d_r[...], t0[...], t1[...])
    hid_o[...] = hidden
    hg = hg_r[...]
    pre = jnp.concatenate([(hg * sf).astype(BF), (hg * sg).astype(BF)], axis=1)
    pre_o[...] = pre
    past_o[...] = mm_t(pre, t1[...]).astype(BF)


def second_rest(ids, x_r, hid_r, g_r, pre_r, t0, wo, keep_o, send_o, local_o):
    out = (x_r[...].astype(F32) + mm(hid_r[...], wo[...])).astype(BF)
    keep, send = halves(ids[0], out)
    keep_o[...] = keep
    send_o[...] = send
    local_o[...] = g_r[...].astype(F32) + mm_t(pre_r[...], t0[...])


def third(ids, local_r, arrived_r, slope_r, t0, t1, wo, g_o, pre_o, past_o, now_o):
    g = (local_r[...] + arrived_r[...].astype(F32)).astype(BF)
    g_o[...] = g
    hg = mm_t(g, wo[...])
    width = g.shape[1]
    pre = jnp.concatenate(
        [(hg * slope_r[:, :width]).astype(BF), (hg * slope_r[:, width:]).astype(BF)], axis=1
    )
    pre_o[...] = pre
    past_o[...] = mm_t(pre, t1[...]).astype(past_o.dtype)
    now_o[...] = g.astype(F32) + mm_t(pre, t0[...])


def last(ids, now_r, past_r, keep_o, send_o):
    keep, send = halves(ids[0], (now_r[...] + past_r[...].astype(F32)).astype(BF))
    keep_o[...] = keep
    send_o[...] = send


def weight_body(scale, steps, ids, *refs):
    (xa, da, pa, ha, ga, xb, db, pb, hb, gb, keep_o, send_o, now, past, outg) = refs
    step = pl.program_id(0)

    @pl.when(step == 0)
    def _():
        now[...] = jnp.zeros_like(now)
        past[...] = jnp.zeros_like(past)
        outg[...] = jnp.zeros_like(outg)

    now[...] += mm_rows(xa[...], pa[...]) + mm_rows(xb[...], pb[...])
    past[...] += mm_rows(da[...], pa[...]) + mm_rows(db[...], pb[...])
    outg[...] += mm_rows(ha[...], ga[...]) + mm_rows(hb[...], gb[...])

    @pl.when(step == steps - 1)
    def _():
        channels = outg.shape[0]
        parts = [r[:, k * channels : (k + 1) * channels] for r in (now, past) for k in (0, 1)]
        parts.append(outg[...])
        for position, part in enumerate(parts):
            keep, send = halves(ids[0], part * scale)
            keep_o[pl.ds(position * channels, channels), :] = keep
            send_o[pl.ds(position * channels, channels), :] = send.astype(BF)


def split_body(parts, ids, keep_r, arrived_r, own_o, *rest):
    outs, total = rest[:-1], rest[-1]
    me = ids[1]
    total[...] = keep_r[...] + arrived_r[...].astype(F32)
    rows = own_o.shape[0]
    own_o[...] = total[pl.ds(pl.multiple_of(me * rows, rows), rows), :]
    for d in range(1, parts):
        place = lax.rem(me + d, parts) * rows
        outs[d - 1][...] = total[pl.ds(pl.multiple_of(place, rows), rows), :].astype(BF)


def sum_body(ids, own_r, *rest):
    total = own_r[...]
    for r in rest[:-1]:
        total = total + r[...].astype(F32)
    rest[-1][...] = total.astype(BF)


def place_body(parts, ids, own_r, *rest):
    me = ids[1]
    out = rest[-1]
    rows = own_r.shape[0]
    out[pl.ds(pl.multiple_of(me * rows, rows), rows), :] = own_r[...].astype(F32)
    for d in range(1, parts):
        place = lax.rem(me + parts - d, parts) * rows
        out[pl.ds(pl.multiple_of(place, rows), rows), :] = rest[d - 1][...].astype(F32)


def moved_by(values, distance):
    devices = range(lax.axis_size("tm"))
    return lax.ppermute(
        values, "tm", [(i, i + distance) for i in devices if i + distance in devices]
    )


def turned(values, distance):
    size = lax.axis_size("tm")
    return lax.ppermute(values, "tm", [(i, (i + distance) % size) for i in range(size)])


def swapped(values):
    return lax.ppermute(values, "chan", [(0, 1), (1, 0)])


def reduced(ids, keep, arrived):
    parts = lax.axis_size("tm")
    rows, cols = keep.shape
    if parts != 8:
        return lax.psum(keep + arrived.astype(F32), "tm")
    piece = rows // parts
    split = call(
        functools.partial(split_body, parts),
        ids,
        (1,),
        [whole(keep), whole(arrived)],
        [((piece, cols), F32, (piece, cols), fixed_map)]
        + [((piece, cols), BF, (piece, cols), fixed_map)] * (parts - 1),
        [pltpu.VMEM((rows, cols), F32)],
        moved=rows * cols * 8,
    )
    got = [turned(split[d], d) for d in range(1, parts)]
    (total,) = call(
        sum_body,
        ids,
        (1,),
        [whole(split[0])] + [whole(g) for g in got],
        [((piece, cols), BF, (piece, cols), fixed_map)],
        moved=rows * cols * 2,
    )
    back = [turned(total, d) for d in range(1, parts)]
    (result,) = call(
        functools.partial(place_body, parts),
        ids,
        (1,),
        [whole(total)] + [whole(b) for b in back],
        [((rows, cols), F32, (rows, cols), fixed_map)],
        moved=rows * cols * 6,
    )
    return result


def assembled(core, keep_a, got_a, keep_b, got_b):
    first = core == 0
    pieces = []
    for keep, got in ((keep_a, got_a), (keep_b, got_b)):
        pieces += [jnp.where(first, keep, got), jnp.where(first, got, keep)]
    return jnp.concatenate(pieces, axis=0)


def on_device(signal, cotangent, conv_weight, out_weight):
    rows, half_width = signal.shape
    channels = conv_weight.shape[2]
    quarter = rows // 4
    scale = 1.0 / math.sqrt(rows * lax.axis_size("tm"))
    core = lax.axis_index("chan")
    ids = jnp.stack([core, lax.axis_index("tm")]).astype(jnp.int32)
    taps = conv_weight.transpose(0, 1, 2, 3, 4).reshape(2, 2, channels, 2 * channels)
    t00, t01, t10, t11 = taps[0, 0], taps[0, 1], taps[1, 0], taps[1, 1]
    wo0, wo1 = out_weight[0], out_weight[1]
    blk = quarter // 4
    steps = quarter // blk
    wide = 2 * channels

    signal_other = swapped(signal)
    same = lax.dynamic_slice_in_dim(signal, 2 * quarter + core * quarter, quarter, 0)
    cross = lax.dynamic_slice_in_dim(signal, 2 * quarter + (1 - core) * quarter, quarter, 0)
    halo_own = moved_by(same, 1)
    size = lax.axis_size("tm")
    halo_other = lax.ppermute(
        cross,
        ("tm", "chan"),
        [(2 * i + c, 2 * (i + 1) + 1 - c) for i in range(size - 1) for c in (0, 1)],
    )
    cot_other = swapped(cotangent)

    def local_rows(array, half):
        return (array, (blk, half_width), lambda i, s: ((half * 2 + s[0]) * steps + i, 0))

    flop1 = 2 * quarter * (wide * wide + channels * channels)
    x_b, x_a, x1_b, hid0_b, slope_b = call(
        first_b,
        ids,
        (steps,),
        [local_rows(signal, 1), local_rows(signal_other, 1), local_rows(signal, 0), local_rows(signal_other, 0)]
        + [whole(t00), whole(t01), whole(wo0)],
        [out_rows(quarter, channels, BF, blk)] * 4 + [out_rows(quarter, wide, F32, blk)],
        flops=flop1,
        moved=quarter * channels * 20,
    )
    x1_b_past = moved_by(x1_b, 2)
    x_h, x1_a, hid0_a, slope_a = call(
        first_a,
        ids,
        (steps,),
        [by_rows(x_a, blk), by_rows(halo_own, blk), by_rows(halo_other, blk)]
        + [whole(t00), whole(t01), whole(wo0)],
        [out_rows(quarter, channels, BF, blk)] * 3 + [out_rows(quarter, wide, F32, blk)],
        flops=flop1,
        moved=quarter * channels * 18,
    )
    x1_a_past = moved_by(x1_a, 2)

    def cot_half(half):
        return call(
            cot_body,
            ids,
            (steps,),
            [local_rows(cotangent, half), local_rows(cot_other, half), whole(wo1)],
            [out_rows(quarter, channels, BF, blk), out_rows(quarter, channels, F32, blk)],
            flops=2 * quarter * channels * channels,
            moved=quarter * channels * 8,
        )

    cot_b, hg_b = cot_half(1)
    cot_a, hg_a = cot_half(0)

    def second_half(x1, past, hg):
        return call(
            second,
            ids,
            (steps,),
            [by_rows(x1, blk), by_rows(past, blk), by_rows(hg, blk), whole(t10), whole(t11)],
            [out_rows(quarter, wide, BF, blk)] + [out_rows(quarter, channels, BF, blk)] * 2,
            flops=2 * quarter * wide * (wide + channels),
            moved=quarter * channels * 16,
        )

    pre1_b, to_past_b, hid1_b = second_half(x1_b, x1_b_past, hg_b)
    from_next_b = moved_by(to_past_b, -2)
    pre1_a, to_past_a, hid1_a = second_half(x1_a, x1_a_past, hg_a)
    from_next_a = moved_by(to_past_a, -2)

    def rest_half(x1, hid1, cot, pre1):
        return call(
            second_rest,
            ids,
            (steps,),
            [by_rows(x1, blk), by_rows(hid1, blk), by_rows(cot, blk), by_rows(pre1, blk), whole(t10), whole(wo1)],
            [out_rows(quarter, half_width, BF, blk)] * 2 + [out_rows(quarter, channels, F32, blk)],
            flops=2 * quarter * channels * (wide + channels),
            moved=quarter * channels * 16,
        )

    out_keep_b, out_send_b, local_b = rest_half(x1_b, hid1_b, cot_b, pre1_b)
    out_keep_a, out_send_a, local_a = rest_half(x1_a, hid1_a, cot_a, pre1_a)
    output = assembled(core, out_keep_a, swapped(out_send_a), out_keep_b, swapped(out_send_b))

    def weights(*arrays):
        count = 5 * channels
        return call(
            functools.partial(weight_body, scale, steps),
            ids,
            (steps,),
            [by_rows(a, blk) for a in arrays],
            [((count, half_width), F32, (count, half_width), fixed_map), ((count, half_width), BF, (count, half_width), fixed_map)],
            [pltpu.VMEM((channels, wide), F32)] * 2 + [pltpu.VMEM((channels, channels), F32)],
            flops=4 * quarter * channels * (2 * wide + channels),
            moved=quarter * channels * 24,
        )

    keep1, send1 = weights(
        x1_a, x1_a_past, pre1_a, hid1_a, cot_a, x1_b, x1_b_past, pre1_b, hid1_b, cot_b
    )
    grads1 = reduced(ids, keep1, swapped(send1))

    def third_half(local, arrived, slope, kind):
        return call(
            third,
            ids,
            (steps,),
            [by_rows(local, blk), by_rows(arrived, blk), by_rows(slope, blk), whole(t00), whole(t01), whole(wo0)],
            [
                out_rows(quarter, channels, BF, blk),
                out_rows(quarter, wide, BF, blk),
                out_rows(quarter, channels, kind, blk),
                out_rows(quarter, channels, F32, blk),
            ],
            flops=2 * quarter * channels * (2 * wide + channels),
            moved=quarter * channels * 26,
        )

    g1_b, pre0_b, past_b, now_b = third_half(local_b, from_next_b, slope_b, F32)
    g1_a, pre0_a, past_a, now_a = third_half(local_a, from_next_a, slope_a, BF)
    ahead_b = moved_by(past_a, -1)
    keep0, send0 = weights(
        x_a, x_h, pre0_a, hid0_a, g1_a, x_b, x_a, pre0_b, hid0_b, g1_b
    )
    grads0 = reduced(ids, keep0, swapped(send0))

    def last_half(now, past):
        return call(
            last,
            ids,
            (steps,),
            [by_rows(now, blk), by_rows(past, blk)],
            [out_rows(quarter, half_width, BF, blk)] * 2,
            moved=quarter * channels * 10,
        )

    in_keep_a, in_send_a = last_half(now_a, past_b)
    in_keep_b, in_send_b = last_half(now_b, ahead_b)
    in_grad = assembled(core, in_keep_a, swapped(in_send_a), in_keep_b, swapped(in_send_b))

    grads = jnp.stack([grads0, grads1]).reshape(2, 5, channels, half_width)
    conv_grad = grads[:, :4].reshape(2, 2, 2, channels, half_width).transpose(0, 1, 3, 2, 4)
    return output, in_grad, conv_grad, grads[:, 4]


def solution(mesh):
    placed = (P(("groups", "tm"), "chan"), P(("groups", "tm"), "chan"), P(), P())
    return jax.shard_map(
        on_device,
        mesh=mesh,
        in_specs=placed,
        out_specs=(
            P(("groups", "tm"), "chan"),
            P(("groups", "tm"), "chan"),
            P("groups", None, None, None, "chan"),
            P("groups", None, "chan"),
        ),
        check_vma=False,
    )
```

```python
import functools
import math

import jax
import jax.numpy as jnp
from jax import lax
from jax.experimental import pallas as pl
from jax.experimental.pallas import tpu as pltpu
from jax.sharding import PartitionSpec as P

BF = jnp.bfloat16
F32 = jnp.float32
VMEM_LIMIT = 24 * 1024 * 1024
CHUNK = 256


def mm(a, b):
    return jnp.dot(a, b, preferred_element_type=F32)


def mm_t(a, b):
    return lax.dot_general(a, b, (((1,), (1,)), ((), ())), preferred_element_type=F32)


def mm_rows(a, b):
    return lax.dot_general(a, b, (((0,), (0,)), ((), ())), preferred_element_type=F32)


def ordered(core, own, other):
    first = core == 0
    return jnp.concatenate(
        [jnp.where(first, own, other), jnp.where(first, other, own)], axis=1
    )


def halves(core, values):
    width = values.shape[1] // 2
    low, high = values[:, :width], values[:, width:]
    first = core == 0
    return jnp.where(first, low, high), jnp.where(first, high, low)


def chunks(ref):
    return [pl.ds(r, CHUNK) for r in range(0, ref.shape[0], CHUNK)]


def run(body, ids, ins, outs, scratch=(), after=()):
    count = len(ins)

    def kernel(ids_ref, *refs):
        body(ids_ref, *refs[:count], *refs[count + len(after) :])

    return pl.pallas_call(
        kernel,
        in_specs=[pl.BlockSpec(memory_space=pltpu.SMEM)]
        + [pl.BlockSpec(memory_space=pltpu.VMEM)] * count
        + [pl.BlockSpec(memory_space=pl.ANY)] * len(after),
        out_specs=[pl.BlockSpec(memory_space=pltpu.VMEM)] * len(outs),
        out_shape=[jax.ShapeDtypeStruct(shape, kind) for shape, kind in outs],
        scratch_shapes=list(scratch),
        compiler_params=pltpu.CompilerParams(vmem_limit_bytes=VMEM_LIMIT),
        cost_estimate=pl.CostEstimate(flops=1, bytes_accessed=1, transcendentals=0),
    )(ids, *ins, *after)


def gated(x, delayed, taps, layer):
    width = x.shape[1]
    preact = mm(x, taps[layer, 0]) + mm(delayed, taps[layer, 1])
    filt = jnp.tanh(preact[:, :width])
    gate = 0.5 * jnp.tanh(0.5 * preact[:, width:]) + 0.5
    hidden = (filt * gate).astype(BF)
    return hidden, gate * (1.0 - filt * filt), filt * gate * (1.0 - gate)


def join_body(ids, own, other, a_o, b_o):
    core = ids[0]
    count = a_o.shape[0]
    for half, out in ((0, a_o), (1, b_o)):
        for rows in chunks(out):
            place = pl.ds(pl.multiple_of((half * 2 + core) * count + rows.start, CHUNK), CHUNK)
            out[rows, :] = ordered(core, own[place, :], other[place, :])


def cot_body(ids, own, other, wo, a_o, b_o, ha_o, hb_o):
    join_body(ids, own, other, a_o, b_o)
    for g_r, h_r in ((a_o, ha_o), (b_o, hb_o)):
        for rows in chunks(g_r):
            h_r[rows, :] = mm_t(g_r[rows, :], wo[1])


def first_body(ids, x_r, d_r, taps, wo, x1_o, hid_o, slope_o):
    width = x_r.shape[1]
    for rows in chunks(x_r):
        x = x_r[rows, :]
        hidden, sf, sg = gated(x, d_r[rows, :], taps, 0)
        hid_o[rows, :] = hidden
        slope_o[rows, :width] = sf
        slope_o[rows, width:] = sg
        x1_o[rows, :] = (x.astype(F32) + mm(hidden, wo[0])).astype(BF)


def second_body(ids, x_r, d_r, hg_r, taps, pre_o, past_o, hid_o):
    for rows in chunks(x_r):
        hidden, sf, sg = gated(x_r[rows, :], d_r[rows, :], taps, 1)
        hid_o[rows, :] = hidden
        hg = hg_r[rows, :]
        pre = jnp.concatenate([(hg * sf).astype(BF), (hg * sg).astype(BF)], axis=1)
        pre_o[rows, :] = pre
        past_o[rows, :] = mm_t(pre, taps[1, 1]).astype(BF)


def rest_body(ids, x_r, hid_r, g_r, pre_r, taps, wo, keep_o, send_o, local_o):
    for rows in chunks(x_r):
        out = (x_r[rows, :].astype(F32) + mm(hid_r[rows, :], wo[1])).astype(BF)
        keep, send = halves(ids[0], out)
        keep_o[rows, :] = keep
        send_o[rows, :] = send
        local_o[rows, :] = g_r[rows, :].astype(F32) + mm_t(pre_r[rows, :], taps[1, 0])


def third_body(ids, local_r, arrived_r, slope_r, taps, wo, g_o, pre_o, past_o, now_o):
    width = g_o.shape[1]
    for rows in chunks(local_r):
        g = (local_r[rows, :] + arrived_r[rows, :].astype(F32)).astype(BF)
        g_o[rows, :] = g
        hg = mm_t(g, wo[0])
        pre = jnp.concatenate(
            [
                (hg * slope_r[rows, :width]).astype(BF),
                (hg * slope_r[rows, width:]).astype(BF),
            ],
            axis=1,
        )
        pre_o[rows, :] = pre
        past_o[rows, :] = mm_t(pre, taps[0, 1]).astype(past_o.dtype)
        now_o[rows, :] = g.astype(F32) + mm_t(pre, taps[0, 0])


def last_body(ids, now_r, past_r, keep_o, send_o):
    for rows in chunks(now_r):
        keep, send = halves(
            ids[0], (now_r[rows, :] + past_r[rows, :].astype(F32)).astype(BF)
        )
        keep_o[rows, :] = keep
        send_o[rows, :] = send


def assemble_body(ids, keep_a, got_a, keep_b, got_b, out):
    core = ids[0]
    count = keep_a.shape[0]
    for half, keep, got in ((0, keep_a, got_a), (1, keep_b, got_b)):
        own = pl.multiple_of((half * 2 + core) * count, count)
        other = pl.multiple_of((half * 2 + 1 - core) * count, count)
        out[pl.ds(own, count), :] = keep[...]
        out[pl.ds(other, count), :] = got[...]


def weight_body(scale, ids, xa, da, pa, ha, ga, xb, db, pb, hb, gb, keep_o, send_o):
    channels = ha.shape[1]
    pairs = (
        (xa, pa, xb, pb),
        (da, pa, db, pb),
        (ha, ga, hb, gb),
    )
    position = 0
    for la, ra, lb, rb in pairs:
        both = (mm_rows(la[...], ra[...]) + mm_rows(lb[...], rb[...])) * scale
        for k in range(both.shape[1] // channels):
            keep, send = halves(ids[0], both[:, k * channels : (k + 1) * channels])
            keep_o[pl.ds(position * channels, channels), :] = keep
            send_o[pl.ds(position * channels, channels), :] = send.astype(BF)
            position += 1


def gather_sums(channels, keeps, gots, total):
    for layer, (keep, got) in enumerate(zip(keeps, gots)):
        for position in range(5):
            rows = pl.ds(position * channels, channels)
            value = keep[rows, :] + got[rows, :].astype(F32)
            if position < 4:
                tap, k = divmod(position, 2)
                base = (layer * 2 + tap) * 2 * channels + k
                total[pl.ds(base, channels, stride=2), :] = value
            else:
                total[pl.ds((8 + layer) * channels, channels), :] = value


def split_body(parts, ids, keep0, got0, keep1, got1, own_o, *rest):
    outs, total = rest[:-1], rest[-1]
    me = ids[1]
    gather_sums(total.shape[0] // 10, (keep0, keep1), (got0, got1), total)
    rows = own_o.shape[0]
    own_o[...] = total[pl.ds(pl.multiple_of(me * rows, rows), rows), :]
    for d in range(1, parts):
        place = lax.rem(me + d, parts) * rows
        outs[d - 1][...] = total[pl.ds(pl.multiple_of(place, rows), rows), :].astype(BF)


def sum_body(ids, own_r, *rest):
    total = own_r[...]
    for r in rest[:-1]:
        total = total + r[...].astype(F32)
    rest[-1][...] = total.astype(BF)


def place_body(parts, ids, own_r, *rest):
    me = ids[1]
    conv_o, out_o, total = rest[-3:]
    rows = own_r.shape[0]
    total[pl.ds(pl.multiple_of(me * rows, rows), rows), :] = own_r[...].astype(F32)
    for d in range(1, parts):
        place = lax.rem(me + parts - d, parts) * rows
        total[pl.ds(pl.multiple_of(place, rows), rows), :] = rest[d - 1][...].astype(F32)
    count = conv_o.shape[0]
    conv_o[...] = total[:count, :]
    out_o[...] = total[count:, :]


def plain_body(ids, keep0, got0, keep1, got1, total):
    gather_sums(total.shape[0] // 10, (keep0, keep1), (got0, got1), total)


def moved_by(values, distance):
    devices = range(lax.axis_size("tm"))
    return lax.ppermute(
        values, "tm", [(i, i + distance) for i in devices if i + distance in devices]
    )


def turned(values, distance):
    size = lax.axis_size("tm")
    return lax.ppermute(values, "tm", [(i, (i + distance) % size) for i in range(size)])


def swapped(values):
    return lax.ppermute(values, "chan", [(0, 1), (1, 0)])


def reduced(ids, channels, sums, after):
    parts = lax.axis_size("tm")
    cols = sums[0].shape[1]
    rows = 10 * channels
    if parts != 8:
        (total,) = run(plain_body, ids, sums, [((rows, cols), F32)])
        total = lax.psum(total, "tm")
        return total[: 8 * channels], total[8 * channels :]
    piece = rows // parts
    split = run(
        functools.partial(split_body, parts),
        ids,
        sums,
        [((piece, cols), F32)] + [((piece, cols), BF)] * (parts - 1),
        [pltpu.VMEM((rows, cols), F32)],
        after=after,
    )
    got = [turned(split[d], d) for d in range(1, parts)]
    (total,) = run(sum_body, ids, [split[0]] + got, [((piece, cols), BF)])
    back = [turned(total, d) for d in range(1, parts)]
    return run(
        functools.partial(place_body, parts),
        ids,
        [total] + back,
        [((8 * channels, cols), F32), ((2 * channels, cols), F32)],
        [pltpu.VMEM((rows, cols), F32)],
    )


def on_device(signal, cotangent, conv_weight, out_weight):
    rows, half_width = signal.shape
    channels = conv_weight.shape[2]
    quarter = rows // 4
    wide = 2 * channels
    scale = 1.0 / math.sqrt(rows * lax.axis_size("tm"))
    ids = jnp.stack([lax.axis_index("chan"), lax.axis_index("tm")]).astype(jnp.int32)
    taps = conv_weight.reshape(2, 2, channels, wide)
    wo = out_weight

    narrow, broad = (quarter, channels), (quarter, wide)
    half = (quarter, half_width)

    x_a, x_b = run(join_body, ids, [signal, swapped(signal)], [(narrow, BF)] * 2)
    x_h = moved_by(x_b, 1)

    def first(x, delayed, after=()):
        return run(
            first_body, ids, [x, delayed, taps, wo], [(narrow, BF)] * 2 + [(broad, F32)], after=after
        )

    x1_b, hid0_b, slope_b = first(x_b, x_a)
    x1_b_past = moved_by(x1_b, 2)
    cot_a, cot_b, hg_a, hg_b = run(
        cot_body,
        ids,
        [cotangent, swapped(cotangent), wo],
        [(narrow, BF)] * 2 + [(narrow, F32)] * 2,
        after=[x1_b],
    )
    x1_a, hid0_a, slope_a = first(x_a, x_h, after=[cot_a])
    x1_a_past = moved_by(x1_a, 2)

    def second(x1, past, hg, after=()):
        return run(
            second_body,
            ids,
            [x1, past, hg, taps],
            [(broad, BF)] + [(narrow, BF)] * 2,
            after=after,
        )

    def rest(x1, hid1, cot, pre1, after=()):
        return run(
            rest_body,
            ids,
            [x1, hid1, cot, pre1, taps, wo],
            [(half, BF)] * 2 + [(narrow, F32)],
            after=after,
        )

    pre1_b, to_past_b, hid1_b = second(x1_b, x1_b_past, hg_b)
    from_next_b = moved_by(to_past_b, -2)
    out_keep_b, out_send_b, local_b = rest(x1_b, hid1_b, cot_b, pre1_b)
    pre1_a, to_past_a, hid1_a = second(x1_a, x1_a_past, hg_a, after=[local_b])
    from_next_a = moved_by(to_past_a, -2)
    out_keep_a, out_send_a, local_a = rest(x1_a, hid1_a, cot_a, pre1_a)

    def weights(arrays, after=()):
        shape = (5 * channels, half_width)
        return run(
            functools.partial(weight_body, scale),
            ids,
            arrays,
            [(shape, F32), (shape, BF)],
            after=after,
        )

    keep1, send1 = weights(
        [x1_a, x1_a_past, pre1_a, hid1_a, cot_a, x1_b, x1_b_past, pre1_b, hid1_b, cot_b],
        after=[local_a],
    )
    got1 = swapped(send1)
    (output,) = run(
        assemble_body,
        ids,
        [out_keep_a, swapped(out_send_a), out_keep_b, swapped(out_send_b)],
        [((rows, half_width), BF)],
        after=[keep1],
    )

    def third(local, arrived, slope, kind, after=()):
        return run(
            third_body,
            ids,
            [local, arrived, slope, taps, wo],
            [(narrow, BF), (broad, BF), (narrow, kind), (narrow, F32)],
            after=after,
        )

    g1_b, pre0_b, past_b, now_b = third(local_b, from_next_b, slope_b, F32, after=[output])
    g1_a, pre0_a, past_a, now_a = third(local_a, from_next_a, slope_a, BF, after=[g1_b])
    ahead_b = moved_by(past_a, -1)
    keep0, send0 = weights(
        [x_a, x_h, pre0_a, hid0_a, g1_a, x_b, x_a, pre0_b, hid0_b, g1_b]
    )
    got0 = swapped(send0)

    def last(now, past, after=()):
        return run(last_body, ids, [now, past], [(half, BF)] * 2, after=after)

    in_keep_a, in_send_a = last(now_a, past_b, after=[keep0])
    conv_grad, out_grad = reduced(ids, channels, [keep0, got0, keep1, got1], [in_keep_a])
    in_keep_b, in_send_b = last(now_b, ahead_b)
    (in_grad,) = run(
        assemble_body,
        ids,
        [in_keep_a, swapped(in_send_a), in_keep_b, swapped(in_send_b)],
        [((rows, half_width), BF)],
    )
    return (
        output,
        in_grad,
        conv_grad.reshape(2, 2, channels, 2, half_width),
        out_grad.reshape(2, channels, half_width),
    )


def solution(mesh):
    placed = (P(("groups", "tm"), "chan"), P(("groups", "tm"), "chan"), P(), P())
    return jax.shard_map(
        on_device,
        mesh=mesh,
        in_specs=placed,
        out_specs=(
            P(("groups", "tm"), "chan"),
            P(("groups", "tm"), "chan"),
            P("groups", None, None, None, "chan"),
            P("groups", None, "chan"),
        ),
        check_vma=False,
    )
```

```python
import functools
import math

import jax
import jax.numpy as jnp
from jax import lax
from jax.experimental import pallas as pl
from jax.experimental.pallas import tpu as pltpu
from jax.sharding import PartitionSpec as P

BF = jnp.bfloat16
F32 = jnp.float32
VMEM_LIMIT = 24 * 1024 * 1024
CHUNK = 256


def mm(a, b):
    return jnp.dot(a, b, preferred_element_type=F32)


def mm_t(a, b):
    return lax.dot_general(a, b, (((1,), (1,)), ((), ())), preferred_element_type=F32)


def mm_rows(a, b):
    return lax.dot_general(a, b, (((0,), (0,)), ((), ())), preferred_element_type=F32)


def ordered(core, own, other):
    first = core == 0
    return jnp.concatenate(
        [jnp.where(first, own, other), jnp.where(first, other, own)], axis=1
    )


def halves(core, values):
    width = values.shape[1] // 2
    low, high = values[:, :width], values[:, width:]
    first = core == 0
    return jnp.where(first, low, high), jnp.where(first, high, low)


def chunks(ref):
    return [pl.ds(r, CHUNK) for r in range(0, ref.shape[0], CHUNK)]


def run(body, ids, ins, outs, scratch=(), after=()):
    count = len(ins)

    def kernel(ids_ref, *refs):
        body(ids_ref, *refs[:count], *refs[count + len(after) :])

    return pl.pallas_call(
        kernel,
        in_specs=[pl.BlockSpec(memory_space=pltpu.SMEM)]
        + [pl.BlockSpec(memory_space=pltpu.VMEM)] * count
        + [pl.BlockSpec(memory_space=pl.ANY)] * len(after),
        out_specs=[pl.BlockSpec(memory_space=pltpu.VMEM)] * len(outs),
        out_shape=[jax.ShapeDtypeStruct(shape, kind) for shape, kind in outs],
        scratch_shapes=list(scratch),
        compiler_params=pltpu.CompilerParams(vmem_limit_bytes=VMEM_LIMIT),
        cost_estimate=pl.CostEstimate(flops=1, bytes_accessed=1, transcendentals=0),
    )(ids, *ins, *after)


def gated(x, delayed, taps, layer):
    width = x.shape[1]
    preact = mm(x, taps[layer, 0]) + mm(delayed, taps[layer, 1])
    filt = jnp.tanh(preact[:, :width])
    gate = 0.5 * jnp.tanh(0.5 * preact[:, width:]) + 0.5
    hidden = (filt * gate).astype(BF)
    return hidden, gate * (1.0 - filt * filt), filt * gate * (1.0 - gate)


def join_body(ids, own, other, a_o, b_o):
    core = ids[0]
    count = a_o.shape[0]
    for half, out in ((0, a_o), (1, b_o)):
        for rows in chunks(out):
            place = pl.ds(pl.multiple_of((half * 2 + core) * count + rows.start, CHUNK), CHUNK)
            out[rows, :] = ordered(core, own[place, :], other[place, :])


def cot_body(ids, own, other, wo, a_o, b_o, ha_o, hb_o):
    join_body(ids, own, other, a_o, b_o)
    for g_r, h_r in ((a_o, ha_o), (b_o, hb_o)):
        for rows in chunks(g_r):
            h_r[rows, :] = mm_t(g_r[rows, :], wo[1])


def first_body(ids, x_r, d_r, taps, wo, x1_o, hid_o, slope_o):
    width = x_r.shape[1]
    for rows in chunks(x_r):
        x = x_r[rows, :]
        hidden, sf, sg = gated(x, d_r[rows, :], taps, 0)
        hid_o[rows, :] = hidden
        slope_o[rows, :width] = sf
        slope_o[rows, width:] = sg
        x1_o[rows, :] = (x.astype(F32) + mm(hidden, wo[0])).astype(BF)


def pre_grad(hg, sf, sg):
    return jnp.concatenate([(hg * sf).astype(BF), (hg * sg).astype(BF)], axis=1)


def second_body(ids, x_r, d_r, hg_r, taps, pre_o, past_o, hid_o):
    for rows in chunks(x_r):
        hidden, sf, sg = gated(x_r[rows, :], d_r[rows, :], taps, 1)
        hid_o[rows, :] = hidden
        pre = pre_grad(hg_r[rows, :], sf, sg)
        pre_o[rows, :] = pre
        past_o[rows, :] = mm_t(pre, taps[1, 1]).astype(BF)


def rest_body(ids, x_r, hid_r, g_r, pre_r, taps, wo, keep_o, send_o, local_o):
    for rows in chunks(x_r):
        out = (x_r[rows, :].astype(F32) + mm(hid_r[rows, :], wo[1])).astype(BF)
        keep, send = halves(ids[0], out)
        keep_o[rows, :] = keep
        send_o[rows, :] = send
        local_o[rows, :] = g_r[rows, :].astype(F32) + mm_t(pre_r[rows, :], taps[1, 0])


def later_body(ids, x_r, d_r, g_r, taps, wo, term_o):
    for rows in chunks(d_r):
        _, sf, sg = gated(x_r[rows, :], d_r[rows, :], taps, 1)
        pre = pre_grad(mm_t(g_r[rows, :], wo[1]), sf, sg)
        term_o[rows, :] = mm_t(pre, taps[1, 1])


def third_rows(rows, g, slope_r, taps, wo, g_o, pre_o, now_o):
    width = g.shape[1]
    g_o[rows, :] = g
    pre = pre_grad(mm_t(g, wo[0]), slope_r[rows, :width], slope_r[rows, width:])
    pre_o[rows, :] = pre
    now_o[rows, :] = g.astype(F32) + mm_t(pre, taps[0, 0])
    return pre


def past_body(ids, pre_r, taps, past_o):
    for rows in chunks(pre_r):
        past_o[rows, :] = mm_t(pre_r[rows, :], taps[0, 1]).astype(BF)


def third_body(ids, local_r, arrived_r, slope_r, now_a, taps, wo, keep_o, send_o, *outs):
    for rows in chunks(local_r):
        g = (local_r[rows, :] + arrived_r[rows, :].astype(F32)).astype(BF)
        pre = third_rows(rows, g, slope_r, taps, wo, *outs)
        keep, send = halves(ids[0], (now_a[rows, :] + mm_t(pre, taps[0, 1])).astype(BF))
        keep_o[rows, :] = keep
        send_o[rows, :] = send


def both_body(ids, x_r, d_r, g_r, hg_r, term_r, slope_r, taps, wo, *outs):
    pre1_o, hid_o, keep_o, send_o = outs[:4]
    for rows in chunks(x_r):
        x = x_r[rows, :]
        hidden, sf, sg = gated(x, d_r[rows, :], taps, 1)
        hid_o[rows, :] = hidden
        pre = pre_grad(hg_r[rows, :], sf, sg)
        pre1_o[rows, :] = pre
        local = g_r[rows, :].astype(F32) + mm_t(pre, taps[1, 0])
        third_rows(rows, (local + term_r[rows, :]).astype(BF), slope_r, taps, wo, *outs[4:])
        out = (x.astype(F32) + mm(hidden, wo[1])).astype(BF)
        keep, send = halves(ids[0], out)
        keep_o[rows, :] = keep
        send_o[rows, :] = send


def last_body(ids, now_r, past_r, keep_o, send_o):
    for rows in chunks(now_r):
        keep, send = halves(
            ids[0], (now_r[rows, :] + past_r[rows, :].astype(F32)).astype(BF)
        )
        keep_o[rows, :] = keep
        send_o[rows, :] = send


def assemble_body(ids, keep_a, got_a, keep_b, got_b, out):
    core = ids[0]
    count = keep_a.shape[0]
    for half, keep, got in ((0, keep_a, got_a), (1, keep_b, got_b)):
        own = pl.multiple_of((half * 2 + core) * count, count)
        other = pl.multiple_of((half * 2 + 1 - core) * count, count)
        out[pl.ds(own, count), :] = keep[...]
        out[pl.ds(other, count), :] = got[...]


def weight_body(scale, ids, xa, da, pa, ha, ga, xb, db, pb, hb, gb, keep_o, send_o):
    channels = ha.shape[1]
    pairs = (
        (xa, pa, xb, pb),
        (da, pa, db, pb),
        (ha, ga, hb, gb),
    )
    position = 0
    for la, ra, lb, rb in pairs:
        both = (mm_rows(la[...], ra[...]) + mm_rows(lb[...], rb[...])) * scale
        for k in range(both.shape[1] // channels):
            keep, send = halves(ids[0], both[:, k * channels : (k + 1) * channels])
            keep_o[pl.ds(position * channels, channels), :] = keep
            send_o[pl.ds(position * channels, channels), :] = send.astype(BF)
            position += 1


def gather_sums(keep, got, total):
    channels = total.shape[0] // 5
    for position in range(5):
        rows = pl.ds(position * channels, channels)
        value = keep[rows, :] + got[rows, :].astype(F32)
        if position < 4:
            tap, k = divmod(position, 2)
            total[pl.ds(tap * 2 * channels + k, channels, stride=2), :] = value
        else:
            total[rows, :] = value


def split_body(ids, keep, got, own_o, send_o, total):
    gather_sums(keep, got, total)
    rows = own_o.shape[0]
    side = ids[1] % 2
    own_o[...] = total[pl.ds(pl.multiple_of(side * rows, rows), rows), :]
    send_o[...] = total[pl.ds(pl.multiple_of((1 - side) * rows, rows), rows), :].astype(BF)


def place_body(ids, own0, got0, own1, got1, conv_o, out_o, total):
    rows = own0.shape[0]
    conv_rows = conv_o.shape[0] // 2
    out_rows = out_o.shape[0] // 2
    side = ids[1] % 2
    for layer, (own, got) in enumerate(((own0, got0), (own1, got1))):
        total[pl.ds(pl.multiple_of(side * rows, rows), rows), :] = own[...].astype(F32)
        total[pl.ds(pl.multiple_of((1 - side) * rows, rows), rows), :] = got[...].astype(F32)
        conv_o[pl.ds(layer * conv_rows, conv_rows), :] = total[:conv_rows, :]
        out_o[pl.ds(layer * out_rows, out_rows), :] = total[conv_rows:, :]


def plain_body(ids, keep, got, total):
    gather_sums(keep, got, total)


def moved_by(values, distance):
    devices = range(lax.axis_size("tm"))
    return lax.ppermute(
        values, "tm", [(i, i + distance) for i in devices if i + distance in devices]
    )


def crossed(values, bit):
    return lax.ppermute(values, "tm", [(i, i ^ bit) for i in range(lax.axis_size("tm"))])


def swapped(values):
    return lax.ppermute(values, "chan", [(0, 1), (1, 0)])


def rounded(values):
    return lax.reduce_precision(values, 8, 7).astype(BF)


def add_body(ids, own, got, total_o):
    total_o[...] = (own[...] + got[...].astype(F32)).astype(BF)


def two_powers():
    size = lax.axis_size("tm")
    return size > 1 and not size & (size - 1)


def split_sums(ids, keep, got, after=()):
    rows, cols = keep.shape
    if not two_powers():
        return run(plain_body, ids, [keep, got], [((rows, cols), F32)])
    return run(
        split_body,
        ids,
        [keep, got],
        [((rows // 2, cols), F32), ((rows // 2, cols), BF)],
        [pltpu.VMEM((rows, cols), F32)],
        after=after,
    )


def reduced(ids, parts, after=()):
    if not two_powers():
        return (lax.psum(parts[0], "tm"),)
    own, send = parts
    (total,) = run(add_body, ids, [own, crossed(send, 1)], [(own.shape, BF)], after=after)
    bit = 2
    while bit < lax.axis_size("tm"):
        total = rounded(total.astype(F32) + crossed(total, bit).astype(F32))
        bit *= 2
    return total, crossed(total, 1)


def placed_sums(ids, channels, layers):
    if not two_powers():
        both = jnp.concatenate(layers[0] + layers[1]).reshape(2, 5 * channels, -1)
        return both[:, : 4 * channels], both[:, 4 * channels :]
    cols = layers[0][0].shape[1]
    return run(
        place_body,
        ids,
        [array for layer in layers for array in layer],
        [((8 * channels, cols), F32), ((2 * channels, cols), F32)],
        [pltpu.VMEM((5 * channels, cols), F32)],
    )


def on_device(signal, cotangent, conv_weight, out_weight):
    rows, half_width = signal.shape
    channels = conv_weight.shape[2]
    quarter = rows // 4
    wide = 2 * channels
    scale = 1.0 / math.sqrt(rows * lax.axis_size("tm"))
    later = 2
    ids = jnp.stack([lax.axis_index("chan"), lax.axis_index("tm")]).astype(jnp.int32)
    taps = conv_weight.reshape(2, 2, channels, wide)
    wo = out_weight

    narrow, broad = (quarter, channels), (quarter, wide)
    half = (quarter, half_width)
    third_outs = [(narrow, BF), (broad, BF), (narrow, F32)]

    x_a, x_b = run(
        join_body, ids, [signal, swapped(signal)], [(narrow, BF)] * 2, after=[taps]
    )
    x_h = moved_by(x_b, 1)
    first_outs = [(narrow, BF)] * 2 + [(broad, F32)]
    x1_b, hid0_b, slope_b = run(
        first_body, ids, [x_b, x_a, taps, wo], first_outs
    )
    x1_b_past = moved_by(x1_b, later)
    cot_a, cot_b, hg_a, hg_b = run(
        cot_body,
        ids,
        [cotangent, swapped(cotangent), wo],
        [(narrow, BF)] * 2 + [(narrow, F32)] * 2,
        after=[x1_b],
    )
    cot_a_later = moved_by(cot_a, -later)
    x1_a, hid0_a, slope_a = run(
        first_body, ids, [x_a, x_h, taps, wo], first_outs, after=[cot_a]
    )
    x1_a_later = moved_by(x1_a, -later)
    x1_a_past = moved_by(x1_a, later)

    pre1_b, to_past_b, hid1_b = run(
        second_body,
        ids,
        [x1_b, x1_b_past, hg_b, taps],
        [(broad, BF)] + [(narrow, BF)] * 2,
        after=[x1_a],
    )
    from_next_b = moved_by(to_past_b, -later)
    out_keep_b, out_send_b, local_b = run(
        rest_body,
        ids,
        [x1_b, hid1_b, cot_b, pre1_b, taps, wo],
        [(half, BF)] * 2 + [(narrow, F32)],
    )
    (term_a,) = run(
        later_body,
        ids,
        [x1_a_later, x1_a, cot_a_later, taps, wo],
        [(narrow, F32)],
        after=[local_b],
    )
    pre1_a, hid1_a, out_keep_a, out_send_a, g1_a, pre0_a, now_a = run(
        both_body,
        ids,
        [x1_a, x1_a_past, cot_a, hg_a, term_a, slope_a, taps, wo],
        [(broad, BF), (narrow, BF), (half, BF), (half, BF)] + third_outs,
    )

    def weights(arrays, after=()):
        shape = (5 * channels, half_width)
        return run(
            functools.partial(weight_body, scale),
            ids,
            arrays,
            [(shape, F32), (shape, BF)],
            after=after,
        )

    keep1, send1 = weights(
        [x1_a, x1_a_past, pre1_a, hid1_a, cot_a, x1_b, x1_b_past, pre1_b, hid1_b, cot_b]
    )
    parts1 = split_sums(ids, keep1, swapped(send1))
    (past_a,) = run(past_body, ids, [pre0_a, taps], [(narrow, BF)], after=parts1)
    ahead_b = moved_by(past_a, -1)
    in_keep_a, in_send_a, g1_b, pre0_b, now_b = run(
        third_body,
        ids,
        [local_b, from_next_b, slope_b, now_a, taps, wo],
        [(half, BF)] * 2 + third_outs,
        after=[past_a],
    )
    keep0, send0 = weights(
        [x_a, x_h, pre0_a, hid0_a, g1_a, x_b, x_a, pre0_b, hid0_b, g1_b]
    )
    parts0 = split_sums(ids, keep0, swapped(send0))
    sums1 = reduced(ids, parts1, after=[keep0])
    in_keep_b, in_send_b = run(last_body, ids, [now_b, ahead_b], [(half, BF)] * 2)
    sums0 = reduced(ids, parts0, after=[in_keep_b])
    conv_grad, out_grad = placed_sums(ids, channels, [sums0, sums1])
    (output,) = run(
        assemble_body,
        ids,
        [out_keep_a, swapped(out_send_a), out_keep_b, swapped(out_send_b)],
        [((rows, half_width), BF)],
        after=[in_keep_b],
    )
    (in_grad,) = run(
        assemble_body,
        ids,
        [in_keep_a, swapped(in_send_a), in_keep_b, swapped(in_send_b)],
        [((rows, half_width), BF)],
    )
    return (
        output,
        in_grad,
        conv_grad.reshape(2, 2, channels, 2, half_width),
        out_grad.reshape(2, channels, half_width),
    )


def solution(mesh):
    placed = (P(("groups", "tm"), "chan"), P(("groups", "tm"), "chan"), P(), P())
    return jax.shard_map(
        on_device,
        mesh=mesh,
        in_specs=placed,
        out_specs=(
            P(("groups", "tm"), "chan"),
            P(("groups", "tm"), "chan"),
            P("groups", None, None, None, "chan"),
            P("groups", None, "chan"),
        ),
        check_vma=False,
    )
```

```python
import functools
import math

import jax
import jax.numpy as jnp
from jax import lax
from jax.experimental import pallas as pl
from jax.experimental.pallas import tpu as pltpu
from jax.sharding import PartitionSpec as P

BF = jnp.bfloat16
F32 = jnp.float32
VMEM_LIMIT = 24 * 1024 * 1024
CHUNK = 256


def mm(a, b):
    return jnp.dot(a, b, preferred_element_type=F32)


def mm_t(a, b):
    return lax.dot_general(a, b, (((1,), (1,)), ((), ())), preferred_element_type=F32)


def mm_rows(a, b):
    return lax.dot_general(a, b, (((0,), (0,)), ((), ())), preferred_element_type=F32)


def ordered(core, own, other):
    first = core == 0
    return jnp.concatenate(
        [jnp.where(first, own, other), jnp.where(first, other, own)], axis=1
    )


def halves(core, values):
    width = values.shape[1] // 2
    low, high = values[:, :width], values[:, width:]
    first = core == 0
    return jnp.where(first, low, high), jnp.where(first, high, low)


def chunks(ref):
    return [pl.ds(r, CHUNK) for r in range(0, ref.shape[0], CHUNK)]


class Place:
    def __getitem__(self, axis):
        return lax.axis_index(("chan", "tm")[axis])


def run(body, ids, ins, outs, scratch=(), after=()):
    count = len(ins)

    def kernel(*refs):
        body(ids, *refs[:count], *refs[count + len(after) :])

    return pl.pallas_call(
        kernel,
        in_specs=[pl.BlockSpec(memory_space=pltpu.VMEM)] * count
        + [pl.BlockSpec(memory_space=pl.ANY)] * len(after),
        out_specs=[pl.BlockSpec(memory_space=pltpu.VMEM)] * len(outs),
        out_shape=[jax.ShapeDtypeStruct(shape, kind) for shape, kind in outs],
        scratch_shapes=list(scratch),
        compiler_params=pltpu.CompilerParams(vmem_limit_bytes=VMEM_LIMIT),
        cost_estimate=pl.CostEstimate(flops=1, bytes_accessed=1, transcendentals=0),
    )(*ins, *after)


def gated(x, delayed, taps, layer):
    width = x.shape[1]
    preact = mm(x, taps[layer, 0]) + mm(delayed, taps[layer, 1])
    filt = jnp.tanh(preact[:, :width])
    gate = 0.5 * jnp.tanh(0.5 * preact[:, width:]) + 0.5
    hidden = (filt * gate).astype(BF)
    return hidden, gate * (1.0 - filt * filt), filt * gate * (1.0 - gate)


def gather_body(ids, own, other, a_o, b_o):
    core = ids[0]
    count = a_o.shape[0]
    for half, out in ((0, a_o), (1, b_o)):
        for rows in chunks(out):
            place = pl.ds(pl.multiple_of((half * 2 + core) * count + rows.start, CHUNK), CHUNK)
            out[rows, :] = ordered(core, own[place, :], other[place, :])


def cot_body(ids, own, other, wo, a_o, b_o, ha_o, hb_o):
    gather_body(ids, own, other, a_o, b_o)
    for g_r, h_r in ((a_o, ha_o), (b_o, hb_o)):
        for rows in chunks(g_r):
            h_r[rows, :] = mm_t(g_r[rows, :], wo[1])


def first_body(ids, x_r, d_r, taps, wo, x1_o, hid_o, slope_o):
    width = x_r.shape[1]
    for rows in chunks(x_r):
        x = x_r[rows, :]
        hidden, sf, sg = gated(x, d_r[rows, :], taps, 0)
        hid_o[rows, :] = hidden
        slope_o[rows, :width] = sf
        slope_o[rows, width:] = sg
        x1_o[rows, :] = (x.astype(F32) + mm(hidden, wo[0])).astype(BF)


def pre_grad(hg, sf, sg):
    return jnp.concatenate([(hg * sf).astype(BF), (hg * sg).astype(BF)], axis=1)


def second_body(ids, x_r, d_r, hg_r, taps, pre_o, past_o, hid_o):
    for rows in chunks(x_r):
        hidden, sf, sg = gated(x_r[rows, :], d_r[rows, :], taps, 1)
        hid_o[rows, :] = hidden
        pre = pre_grad(hg_r[rows, :], sf, sg)
        pre_o[rows, :] = pre
        past_o[rows, :] = mm_t(pre, taps[1, 1]).astype(BF)


def rest_body(ids, x_r, hid_r, g_r, pre_r, taps, wo, keep_o, send_o, local_o):
    for rows in chunks(x_r):
        out = (x_r[rows, :].astype(F32) + mm(hid_r[rows, :], wo[1])).astype(BF)
        keep, send = halves(ids[0], out)
        keep_o[rows, :] = keep
        send_o[rows, :] = send
        local_o[rows, :] = g_r[rows, :].astype(F32) + mm_t(pre_r[rows, :], taps[1, 0])


def later_body(ids, x_r, d_r, g_r, taps, wo, term_o):
    for rows in chunks(d_r):
        _, sf, sg = gated(x_r[rows, :], d_r[rows, :], taps, 1)
        pre = pre_grad(mm_t(g_r[rows, :], wo[1]), sf, sg)
        term_o[rows, :] = mm_t(pre, taps[1, 1])


def third_rows(rows, g, slope_r, taps, wo, g_o, pre_o, now_o):
    width = g.shape[1]
    g_o[rows, :] = g
    pre = pre_grad(mm_t(g, wo[0]), slope_r[rows, :width], slope_r[rows, width:])
    pre_o[rows, :] = pre
    now_o[rows, :] = g.astype(F32) + mm_t(pre, taps[0, 0])
    return pre


def third_body(ids, local_r, arrived_r, slope_r, now_a, taps, wo, keep_o, send_o, *outs):
    for rows in chunks(local_r):
        g = (local_r[rows, :] + arrived_r[rows, :].astype(F32)).astype(BF)
        pre = third_rows(rows, g, slope_r, taps, wo, *outs)
        keep, send = halves(ids[0], (now_a[rows, :] + mm_t(pre, taps[0, 1])).astype(BF))
        keep_o[rows, :] = keep
        send_o[rows, :] = send


def both_body(ids, x_r, d_r, g_r, hg_r, term_r, slope_r, taps, wo, *outs):
    past_o, pre1_o, hid_o, keep_o, send_o = outs[:5]
    for rows in chunks(x_r):
        x = x_r[rows, :]
        hidden, sf, sg = gated(x, d_r[rows, :], taps, 1)
        hid_o[rows, :] = hidden
        pre = pre_grad(hg_r[rows, :], sf, sg)
        pre1_o[rows, :] = pre
        local = g_r[rows, :].astype(F32) + mm_t(pre, taps[1, 0])
        g = (local + term_r[rows, :]).astype(BF)
        pre = third_rows(rows, g, slope_r, taps, wo, *outs[5:])
        past_o[rows, :] = mm_t(pre, taps[0, 1]).astype(BF)
        out = (x.astype(F32) + mm(hidden, wo[1])).astype(BF)
        keep, send = halves(ids[0], out)
        keep_o[rows, :] = keep
        send_o[rows, :] = send


def last_body(size, ids, now_r, past_r, keep_o, send_o):
    ended = ids[1] == size - 1
    for rows in chunks(now_r):
        past = past_r[rows, :].astype(F32)
        past = jnp.where(ended, jnp.zeros_like(past), past)
        keep, send = halves(ids[0], (now_r[rows, :] + past).astype(BF))
        keep_o[rows, :] = keep
        send_o[rows, :] = send


def assemble_body(ids, keep_a, got_a, keep_b, got_b, out):
    core = ids[0]
    count = keep_a.shape[0]
    for half, keep, got in ((0, keep_a, got_a), (1, keep_b, got_b)):
        own = pl.multiple_of((half * 2 + core) * count, count)
        other = pl.multiple_of((half * 2 + 1 - core) * count, count)
        out[pl.ds(own, count), :] = keep[...]
        out[pl.ds(other, count), :] = got[...]


def weight_body(scale, ids, xa, da, pa, ha, ga, xb, db, pb, hb, gb, keep_o, send_o):
    channels = ha.shape[1]
    pairs = (
        (xa, pa, xb, pb),
        (da, pa, db, pb),
        (ha, ga, hb, gb),
    )
    position = 0
    for la, ra, lb, rb in pairs:
        both = (mm_rows(la[...], ra[...]) + mm_rows(lb[...], rb[...])) * scale
        for k in range(both.shape[1] // channels):
            keep, send = halves(ids[0], both[:, k * channels : (k + 1) * channels])
            keep_o[pl.ds(position * channels, channels), :] = keep
            send_o[pl.ds(position * channels, channels), :] = send.astype(BF)
            position += 1


def gather_sums(keep, got, total):
    channels = total.shape[0] // 5
    for position in range(5):
        rows = pl.ds(position * channels, channels)
        value = keep[rows, :] + got[rows, :].astype(F32)
        if position < 4:
            tap, k = divmod(position, 2)
            total[pl.ds(tap * 2 * channels + k, channels, stride=2), :] = value
        else:
            total[rows, :] = value


def side(ids, step):
    return (ids[1] // (1 << step)) % 2


def parted(ids, step, values, own_o, send_o):
    count = own_o.shape[0]
    own = side(ids, step)
    own_o[...] = values(pl.ds(pl.multiple_of(own * count, count), count))
    send_o[...] = values(pl.ds(pl.multiple_of((1 - own) * count, count), count)).astype(BF)


def split_body(ids, keep, got, own_o, send_o, total):
    gather_sums(keep, got, total)
    parted(ids, 0, lambda rows: total[rows, :], own_o, send_o)


def part_body(step, ids, own, got, own_o, send_o):
    parted(
        ids, step, lambda rows: own[rows, :] + got[rows, :].astype(F32), own_o, send_o
    )


def add_body(ids, own, got, total_o):
    total_o[...] = (own[...].astype(F32) + got[...].astype(F32)).astype(BF)


def join_body(ids, first, second, both_o):
    rows = first.shape[0]
    both_o[:rows, :] = first[...]
    both_o[rows:, :] = second[...]


def place_body(cuts, ids, *refs):
    conv_o, out_o = refs[-2:]
    pieces = 1 << cuts
    rows = refs[0].shape[0]
    conv_rows = conv_o.shape[0] // 2
    out_rows = out_o.shape[0] // 2
    for layer in (0, 1):
        held = []
        for ref in refs[layer * (cuts + 1) : (layer + 1) * (cuts + 1)]:
            held += [ref[r : r + rows, :] for r in range(0, ref.shape[0], rows)]
        for bit in range(cuts):
            swap = side(ids, cuts - 1 - bit) == 1
            held = [
                jnp.where(swap, held[i ^ (1 << bit)], held[i]) for i in range(pieces)
            ]
        for i in range(pieces):
            value = held[i].astype(F32)
            start = i * rows
            for k in range(0, rows, 64):
                at = start + k
                if at < conv_rows:
                    conv_o[layer * conv_rows + at : layer * conv_rows + at + 64, :] = value[k : k + 64]
                else:
                    at += layer * out_rows - conv_rows
                    out_o[at : at + 64, :] = value[k : k + 64]


def plain_body(ids, keep, got, total):
    gather_sums(keep, got, total)


def moved_by(values, distance):
    devices = range(lax.axis_size("tm"))
    return lax.ppermute(
        values, "tm", [(i, i + distance) for i in devices if i + distance in devices]
    )


def crossed(values, bit):
    return lax.ppermute(values, "tm", [(i, i ^ bit) for i in range(lax.axis_size("tm"))])


def swapped(values):
    return lax.ppermute(values, "chan", [(0, 1), (1, 0)])


def cuts_of(rows):
    size = lax.axis_size("tm")
    if size < 2 or size & (size - 1) or rows % 64:
        return 0
    return min(2, size.bit_length() - 1)


def split_sums(ids, keep, got, after=()):
    rows, cols = keep.shape
    if not cuts_of(rows):
        return run(plain_body, ids, [keep, got], [((rows, cols), F32)], after=after)
    return run(
        split_body,
        ids,
        [keep, got],
        [((rows // 2, cols), F32), ((rows // 2, cols), BF)],
        [pltpu.VMEM((rows, cols), F32)],
        after=after,
    )


def summed(ids, cuts, step, parts, after):
    if not cuts:
        return parts
    if step < cuts:
        own, send = parts
    else:
        own = send = parts[0]
    got = crossed(send, 1 << step)
    rows, cols = own.shape
    if step + 1 < cuts:
        return run(
            functools.partial(part_body, step + 1),
            ids,
            [own, got],
            [((rows // 2, cols), F32), ((rows // 2, cols), BF)],
            after=after,
        )
    return run(add_body, ids, [own, got], [(own.shape, BF)], after=after)


def spread(ids, cuts, total, after):
    held = [total]
    for step in reversed(range(cuts)):
        both = held[0]
        if len(held) > 1:
            rows, cols = both.shape
            (both,) = run(join_body, ids, held, [((2 * rows, cols), BF)], after=after)
        held.append(crossed(both, 1 << step))
    return held


def placed_sums(ids, channels, cuts, sums0, sums1):
    if not cuts:
        both = jnp.stack([lax.psum(sums[0], "tm") for sums in (sums0, sums1)])
        return both[:, : 4 * channels], both[:, 4 * channels :]
    cols = sums0[0].shape[1]
    late = spread(ids, cuts, sums1[0], [sums0[0]])
    return run(
        functools.partial(place_body, cuts),
        ids,
        spread(ids, cuts, sums0[0], [late[-1]]) + late,
        [((8 * channels, cols), F32), ((2 * channels, cols), F32)],
    )


def on_device(signal, cotangent, conv_weight, out_weight):
    rows, half_width = signal.shape
    channels = conv_weight.shape[2]
    quarter = rows // 4
    wide = 2 * channels
    scale = 1.0 / math.sqrt(rows * lax.axis_size("tm"))
    later = 2
    ids = Place()
    taps = conv_weight.reshape(2, 2, channels, wide)
    wo = out_weight

    narrow, broad = (quarter, channels), (quarter, wide)
    half = (quarter, half_width)
    third_outs = [(narrow, BF), (broad, BF), (narrow, F32)]

    x_a, x_b = run(
        gather_body, ids, [signal, swapped(signal)], [(narrow, BF)] * 2, after=[taps]
    )
    x_h = moved_by(x_b, 1)
    first_outs = [(narrow, BF)] * 2 + [(broad, F32)]
    x1_b, hid0_b, slope_b = run(
        first_body, ids, [x_b, x_a, taps, wo], first_outs
    )
    x1_b_past = moved_by(x1_b, later)
    cot_a, cot_b, hg_a, hg_b = run(
        cot_body,
        ids,
        [cotangent, swapped(cotangent), wo],
        [(narrow, BF)] * 2 + [(narrow, F32)] * 2,
        after=[x1_b],
    )
    cot_a_later = moved_by(cot_a, -later)
    x1_a, hid0_a, slope_a = run(
        first_body, ids, [x_a, x_h, taps, wo], first_outs, after=[cot_a]
    )
    x1_a_later = moved_by(x1_a, -later)
    x1_a_past = moved_by(x1_a, later)

    pre1_b, to_past_b, hid1_b = run(
        second_body,
        ids,
        [x1_b, x1_b_past, hg_b, taps],
        [(broad, BF)] + [(narrow, BF)] * 2,
        after=[x1_a],
    )
    from_next_b = moved_by(to_past_b, -later)
    out_keep_b, out_send_b, local_b = run(
        rest_body,
        ids,
        [x1_b, hid1_b, cot_b, pre1_b, taps, wo],
        [(half, BF)] * 2 + [(narrow, F32)],
    )
    (term_a,) = run(
        later_body,
        ids,
        [x1_a_later, x1_a, cot_a_later, taps, wo],
        [(narrow, F32)],
        after=[local_b],
    )
    past_a, pre1_a, hid1_a, out_keep_a, out_send_a, g1_a, pre0_a, now_a = run(
        both_body,
        ids,
        [x1_a, x1_a_past, cot_a, hg_a, term_a, slope_a, taps, wo],
        [(narrow, BF), (broad, BF), (narrow, BF), (half, BF), (half, BF)] + third_outs,
    )
    size = lax.axis_size("tm")
    ahead_b = lax.ppermute(past_a, "tm", [(i, (i - 1) % size) for i in range(size)])

    def weights(arrays, after=()):
        shape = (5 * channels, half_width)
        return run(
            functools.partial(weight_body, scale),
            ids,
            arrays,
            [(shape, F32), (shape, BF)],
            after=after,
        )

    keep1, send1 = weights(
        [x1_a, x1_a_past, pre1_a, hid1_a, cot_a, x1_b, x1_b_past, pre1_b, hid1_b, cot_b]
    )
    steps = max(1, (lax.axis_size("tm") - 1).bit_length())
    cuts = cuts_of(5 * channels)
    in_keep_a, in_send_a, g1_b, pre0_b, now_b = run(
        third_body,
        ids,
        [local_b, from_next_b, slope_b, now_a, taps, wo],
        [(half, BF)] * 2 + third_outs,
        after=[keep1],
    )
    sums1 = split_sums(ids, keep1, swapped(send1), after=[now_b])
    keep0, send0 = weights(
        [x_a, x_h, pre0_a, hid0_a, g1_a, x_b, x_a, pre0_b, hid0_b, g1_b], after=sums1
    )
    sums0 = split_sums(ids, keep0, swapped(send0))
    sums1 = summed(ids, cuts, 0, sums1, sums0)
    in_keep_b, in_send_b = run(functools.partial(last_body, size), ids, [now_b, ahead_b], [(half, BF)] * 2, after=sums1)
    sums0 = summed(ids, cuts, 0, sums0, [in_keep_b])
    for step in range(1, steps):
        sums1 = summed(ids, cuts, step, sums1, sums0)
        sums0 = summed(ids, cuts, step, sums0, sums1)
    (output,) = run(
        assemble_body,
        ids,
        [out_keep_a, swapped(out_send_a), out_keep_b, swapped(out_send_b)],
        [((rows, half_width), BF)],
        after=[in_keep_b],
    )
    conv_grad, out_grad = placed_sums(ids, channels, cuts, sums0, sums1)
    (in_grad,) = run(
        assemble_body,
        ids,
        [in_keep_a, swapped(in_send_a), in_keep_b, swapped(in_send_b)],
        [((rows, half_width), BF)],
    )
    return (
        output,
        in_grad,
        conv_grad.reshape(2, 2, channels, 2, half_width),
        out_grad.reshape(2, channels, half_width),
    )


def solution(mesh):
    placed = (P(("groups", "tm"), "chan"), P(("groups", "tm"), "chan"), P(), P())
    return jax.shard_map(
        on_device,
        mesh=mesh,
        in_specs=placed,
        out_specs=(
            P(("groups", "tm"), "chan"),
            P(("groups", "tm"), "chan"),
            P("groups", None, None, None, "chan"),
            P("groups", None, "chan"),
        ),
        check_vma=False,
    )
```

```python
import functools
import math

import jax
import jax.numpy as jnp
from jax import lax
from jax.experimental import pallas as pl
from jax.experimental.pallas import tpu as pltpu
from jax.sharding import PartitionSpec as P

BF = jnp.bfloat16
F32 = jnp.float32
VMEM_LIMIT = 24 * 1024 * 1024
CHUNK = 256


def mm(a, b):
    return jnp.dot(a, b, preferred_element_type=F32)


def mm_t(a, b):
    return lax.dot_general(a, b, (((1,), (1,)), ((), ())), preferred_element_type=F32)


def mm_rows(a, b):
    return lax.dot_general(a, b, (((0,), (0,)), ((), ())), preferred_element_type=F32)


def ordered(core, own, other):
    first = core == 0
    return jnp.concatenate(
        [jnp.where(first, own, other), jnp.where(first, other, own)], axis=1
    )


def halves(core, values):
    width = values.shape[1] // 2
    low, high = values[:, :width], values[:, width:]
    first = core == 0
    return jnp.where(first, low, high), jnp.where(first, high, low)


def chunks(ref):
    return [pl.ds(r, CHUNK) for r in range(0, ref.shape[0], CHUNK)]


class Place:
    def __getitem__(self, axis):
        return lax.axis_index(("chan", "tm")[axis])


def run(body, ids, ins, outs, scratch=(), after=()):
    count = len(ins)

    def kernel(*refs):
        body(ids, *refs[:count], *refs[count + len(after) :])

    return pl.pallas_call(
        kernel,
        in_specs=[pl.BlockSpec(memory_space=pltpu.VMEM)] * count
        + [pl.BlockSpec(memory_space=pl.ANY)] * len(after),
        out_specs=[pl.BlockSpec(memory_space=pltpu.VMEM)] * len(outs),
        out_shape=[jax.ShapeDtypeStruct(shape, kind) for shape, kind in outs],
        scratch_shapes=list(scratch),
        compiler_params=pltpu.CompilerParams(vmem_limit_bytes=VMEM_LIMIT),
        cost_estimate=pl.CostEstimate(flops=1, bytes_accessed=1, transcendentals=0),
    )(*ins, *after)


def gated(x, delayed, taps, layer):
    width = x.shape[1]
    preact = mm(x, taps[layer, 0]) + mm(delayed, taps[layer, 1])
    filt = jnp.tanh(preact[:, :width])
    gate = 0.5 * jnp.tanh(0.5 * preact[:, width:]) + 0.5
    hidden = (filt * gate).astype(BF)
    return hidden, gate * (1.0 - filt * filt), filt * gate * (1.0 - gate)


def gather_body(ids, own, other, a_o, b_o):
    core = ids[0]
    count = a_o.shape[0]
    for half, out in ((0, a_o), (1, b_o)):
        for rows in chunks(out):
            place = pl.ds(pl.multiple_of((half * 2 + core) * count + rows.start, CHUNK), CHUNK)
            out[rows, :] = ordered(core, own[place, :], other[place, :])


def cot_body(ids, own, other, wo, a_o, b_o, ha_o, hb_o):
    gather_body(ids, own, other, a_o, b_o)
    for g_r, h_r in ((a_o, ha_o), (b_o, hb_o)):
        for rows in chunks(g_r):
            h_r[rows, :] = mm_t(g_r[rows, :], wo[1])


def first_body(ids, x_r, d_r, taps, wo, x1_o, hid_o, slope_o):
    width = x_r.shape[1]
    for rows in chunks(x_r):
        x = x_r[rows, :]
        hidden, sf, sg = gated(x, d_r[rows, :], taps, 0)
        hid_o[rows, :] = hidden
        slope_o[rows, :width] = sf
        slope_o[rows, width:] = sg
        x1_o[rows, :] = (x.astype(F32) + mm(hidden, wo[0])).astype(BF)


def pre_grad(hg, sf, sg):
    return jnp.concatenate([(hg * sf).astype(BF), (hg * sg).astype(BF)], axis=1)


def second_body(ids, x_r, d_r, hg_r, taps, pre_o, past_o, hid_o):
    for rows in chunks(x_r):
        hidden, sf, sg = gated(x_r[rows, :], d_r[rows, :], taps, 1)
        hid_o[rows, :] = hidden
        pre = pre_grad(hg_r[rows, :], sf, sg)
        pre_o[rows, :] = pre
        past_o[rows, :] = mm_t(pre, taps[1, 1]).astype(BF)


def rest_body(ids, x_r, hid_r, g_r, pre_r, taps, wo, keep_o, send_o, local_o):
    for rows in chunks(x_r):
        out = (x_r[rows, :].astype(F32) + mm(hid_r[rows, :], wo[1])).astype(BF)
        keep, send = halves(ids[0], out)
        keep_o[rows, :] = keep
        send_o[rows, :] = send
        local_o[rows, :] = g_r[rows, :].astype(F32) + mm_t(pre_r[rows, :], taps[1, 0])


def later_body(ids, x_r, d_r, g_r, taps, wo, term_o):
    for rows in chunks(d_r):
        _, sf, sg = gated(x_r[rows, :], d_r[rows, :], taps, 1)
        pre = pre_grad(mm_t(g_r[rows, :], wo[1]), sf, sg)
        term_o[rows, :] = mm_t(pre, taps[1, 1])


def third_rows(rows, g, slope_r, taps, wo, g_o, pre_o, now_o):
    width = g.shape[1]
    g_o[rows, :] = g
    pre = pre_grad(mm_t(g, wo[0]), slope_r[rows, :width], slope_r[rows, width:])
    pre_o[rows, :] = pre
    now_o[rows, :] = g.astype(F32) + mm_t(pre, taps[0, 0])
    return pre


def third_body(ids, local_r, arrived_r, slope_r, now_a, taps, wo, keep_o, send_o, *outs):
    for rows in chunks(local_r):
        g = (local_r[rows, :] + arrived_r[rows, :].astype(F32)).astype(BF)
        pre = third_rows(rows, g, slope_r, taps, wo, *outs)
        keep, send = halves(ids[0], (now_a[rows, :] + mm_t(pre, taps[0, 1])).astype(BF))
        keep_o[rows, :] = keep
        send_o[rows, :] = send


def both_body(ids, x_r, d_r, g_r, hg_r, term_r, slope_r, taps, wo, *outs):
    past_o, pre1_o, hid_o, keep_o, send_o = outs[:5]
    for rows in chunks(x_r):
        x = x_r[rows, :]
        hidden, sf, sg = gated(x, d_r[rows, :], taps, 1)
        hid_o[rows, :] = hidden
        pre = pre_grad(hg_r[rows, :], sf, sg)
        pre1_o[rows, :] = pre
        local = g_r[rows, :].astype(F32) + mm_t(pre, taps[1, 0])
        g = (local + term_r[rows, :]).astype(BF)
        pre = third_rows(rows, g, slope_r, taps, wo, *outs[5:])
        past_o[rows, :] = mm_t(pre, taps[0, 1]).astype(BF)
        out = (x.astype(F32) + mm(hidden, wo[1])).astype(BF)
        keep, send = halves(ids[0], out)
        keep_o[rows, :] = keep
        send_o[rows, :] = send


def last_body(size, ids, now_r, past_r, keep_o, send_o):
    ended = ids[1] == size - 1
    for rows in chunks(now_r):
        past = past_r[rows, :].astype(F32)
        past = jnp.where(ended, jnp.zeros_like(past), past)
        keep, send = halves(ids[0], (now_r[rows, :] + past).astype(BF))
        keep_o[rows, :] = keep
        send_o[rows, :] = send


def assemble_body(ids, keep_a, got_a, keep_b, got_b, out):
    core = ids[0]
    count = keep_a.shape[0]
    for half, keep, got in ((0, keep_a, got_a), (1, keep_b, got_b)):
        own = pl.multiple_of((half * 2 + core) * count, count)
        other = pl.multiple_of((half * 2 + 1 - core) * count, count)
        out[pl.ds(own, count), :] = keep[...]
        out[pl.ds(other, count), :] = got[...]


def weight_body(scale, ids, xa, da, pa, ha, ga, xb, db, pb, hb, gb, keep_o, send_o):
    channels = ha.shape[1]
    pairs = (
        (xa, pa, xb, pb),
        (da, pa, db, pb),
        (ha, ga, hb, gb),
    )
    position = 0
    for la, ra, lb, rb in pairs:
        both = (mm_rows(la[...], ra[...]) + mm_rows(lb[...], rb[...])) * scale
        for k in range(both.shape[1] // channels):
            keep, send = halves(ids[0], both[:, k * channels : (k + 1) * channels])
            keep_o[pl.ds(position * channels, channels), :] = keep
            send_o[pl.ds(position * channels, channels), :] = send.astype(BF)
            position += 1


def gather_sums(keep, got, total):
    channels = total.shape[0] // 5
    for position in range(5):
        rows = pl.ds(position * channels, channels)
        value = keep[rows, :] + got[rows, :].astype(F32)
        if position < 4:
            tap, k = divmod(position, 2)
            total[pl.ds(tap * 2 * channels + k, channels, stride=2), :] = value
        else:
            total[rows, :] = value


def side(ids, step):
    return (ids[1] // (1 << step)) % 2


def parted(ids, step, values, own_o, send_o):
    count = own_o.shape[0]
    own = side(ids, step)
    own_o[...] = values(pl.ds(pl.multiple_of(own * count, count), count))
    send_o[...] = values(pl.ds(pl.multiple_of((1 - own) * count, count), count)).astype(BF)


def split_body(ids, keep, got, own_o, send_o, total):
    gather_sums(keep, got, total)
    parted(ids, 0, lambda rows: total[rows, :], own_o, send_o)


def part_body(step, ids, own, got, own_o, send_o):
    parted(
        ids, step, lambda rows: own[rows, :] + got[rows, :].astype(F32), own_o, send_o
    )


def add_body(ids, own, got, total_o):
    total_o[...] = (own[...].astype(F32) + got[...].astype(F32)).astype(BF)


def join_body(ids, first, second, both_o):
    rows = first.shape[0]
    both_o[:rows, :] = first[...]
    both_o[rows:, :] = second[...]


def place_body(cuts, ids, *refs):
    conv_o, out_o = refs[-2:]
    pieces = 1 << cuts
    rows = refs[0].shape[0]
    conv_rows = conv_o.shape[0] // 2
    out_rows = out_o.shape[0] // 2
    for layer in (0, 1):
        held = []
        for ref in refs[layer * (cuts + 1) : (layer + 1) * (cuts + 1)]:
            held += [ref[r : r + rows, :] for r in range(0, ref.shape[0], rows)]
        for bit in range(cuts):
            swap = side(ids, cuts - 1 - bit) == 1
            held = [
                jnp.where(swap, held[i ^ (1 << bit)], held[i]) for i in range(pieces)
            ]
        for i in range(pieces):
            value = held[i].astype(F32)
            start = i * rows
            for k in range(0, rows, 64):
                at = start + k
                if at < conv_rows:
                    conv_o[layer * conv_rows + at : layer * conv_rows + at + 64, :] = value[k : k + 64]
                else:
                    at += layer * out_rows - conv_rows
                    out_o[at : at + 64, :] = value[k : k + 64]


def plain_body(ids, keep, got, total):
    gather_sums(keep, got, total)


def moved_by(values, distance):
    devices = range(lax.axis_size("tm"))
    return lax.ppermute(
        values, "tm", [(i, i + distance) for i in devices if i + distance in devices]
    )


def crossed(values, bit):
    return lax.ppermute(values, "tm", [(i, i ^ bit) for i in range(lax.axis_size("tm"))])


def swapped(values):
    return lax.ppermute(values, "chan", [(0, 1), (1, 0)])


def cuts_of(rows):
    size = lax.axis_size("tm")
    if size < 2 or size & (size - 1) or rows % 64:
        return 0
    return min(2, size.bit_length() - 1)


def split_sums(ids, keep, got, after=()):
    rows, cols = keep.shape
    if not cuts_of(rows):
        return run(plain_body, ids, [keep, got], [((rows, cols), F32)], after=after)
    return run(
        split_body,
        ids,
        [keep, got],
        [((rows // 2, cols), F32), ((rows // 2, cols), BF)],
        [pltpu.VMEM((rows, cols), F32)],
        after=after,
    )


def summed(ids, cuts, step, parts, after):
    if not cuts:
        return parts
    if step < cuts:
        own, send = parts
    else:
        own = send = parts[0]
    got = crossed(send, 1 << step)
    rows, cols = own.shape
    if step + 1 < cuts:
        return run(
            functools.partial(part_body, step + 1),
            ids,
            [own, got],
            [((rows // 2, cols), F32), ((rows // 2, cols), BF)],
            after=after,
        )
    return run(add_body, ids, [own, got], [(own.shape, BF)], after=after)


def spread(ids, cuts, total, after):
    held = [total]
    for step in reversed(range(cuts)):
        both = held[0]
        if len(held) > 1:
            rows, cols = both.shape
            (both,) = run(join_body, ids, held, [((2 * rows, cols), BF)], after=after)
        held.append(crossed(both, 1 << step))
    return held


def placed_sums(ids, channels, cuts, sums0, sums1):
    if not cuts:
        both = jnp.stack([lax.psum(sums[0], "tm") for sums in (sums0, sums1)])
        return both[:, : 4 * channels], both[:, 4 * channels :]
    cols = sums0[0].shape[1]
    late = spread(ids, cuts, sums1[0], [sums0[0]])
    return run(
        functools.partial(place_body, cuts),
        ids,
        spread(ids, cuts, sums0[0], [late[-1]]) + late,
        [((8 * channels, cols), F32), ((2 * channels, cols), F32)],
    )


def on_device(signal, cotangent, conv_weight, out_weight):
    rows, half_width = signal.shape
    channels = conv_weight.shape[2]
    quarter = rows // 4
    wide = 2 * channels
    scale = 1.0 / math.sqrt(rows * lax.axis_size("tm"))
    later = 2
    ids = Place()
    taps = conv_weight.reshape(2, 2, channels, wide)
    wo = out_weight

    narrow, broad = (quarter, channels), (quarter, wide)
    half = (quarter, half_width)
    third_outs = [(narrow, BF), (broad, BF), (narrow, F32)]

    x_a, x_b = run(
        gather_body, ids, [signal, swapped(signal)], [(narrow, BF)] * 2, after=[taps]
    )
    x_h = moved_by(x_b, 1)
    first_outs = [(narrow, BF)] * 2 + [(broad, F32)]
    cot_a, cot_b, hg_a, hg_b = run(
        cot_body,
        ids,
        [cotangent, swapped(cotangent), wo],
        [(narrow, BF)] * 2 + [(narrow, F32)] * 2,
        after=[x_b],
    )
    cot_a_later = moved_by(cot_a, -later)
    x1_b, hid0_b, slope_b = run(
        first_body, ids, [x_b, x_a, taps, wo], first_outs, after=[cot_a]
    )
    x1_b_past = moved_by(x1_b, later)
    x1_a, hid0_a, slope_a = run(
        first_body, ids, [x_a, x_h, taps, wo], first_outs, after=[x1_b]
    )
    x1_a_later = moved_by(x1_a, -later)
    x1_a_past = moved_by(x1_a, later)

    pre1_b, to_past_b, hid1_b = run(
        second_body,
        ids,
        [x1_b, x1_b_past, hg_b, taps],
        [(broad, BF)] + [(narrow, BF)] * 2,
        after=[x1_a, cot_a_later],
    )
    from_next_b = moved_by(to_past_b, -later)
    out_keep_b, out_send_b, local_b = run(
        rest_body,
        ids,
        [x1_b, hid1_b, cot_b, pre1_b, taps, wo],
        [(half, BF)] * 2 + [(narrow, F32)],
    )
    (term_a,) = run(
        later_body,
        ids,
        [x1_a_later, x1_a, cot_a_later, taps, wo],
        [(narrow, F32)],
        after=[local_b],
    )
    past_a, pre1_a, hid1_a, out_keep_a, out_send_a, g1_a, pre0_a, now_a = run(
        both_body,
        ids,
        [x1_a, x1_a_past, cot_a, hg_a, term_a, slope_a, taps, wo],
        [(narrow, BF), (broad, BF), (narrow, BF), (half, BF), (half, BF)] + third_outs,
    )
    size = lax.axis_size("tm")
    ahead_b = moved_by(past_a, -1)

    def weights(arrays, after=()):
        shape = (5 * channels, half_width)
        return run(
            functools.partial(weight_body, scale),
            ids,
            arrays,
            [(shape, F32), (shape, BF)],
            after=after,
        )

    keep1, send1 = weights(
        [x1_a, x1_a_past, pre1_a, hid1_a, cot_a, x1_b, x1_b_past, pre1_b, hid1_b, cot_b]
    )
    steps = max(1, (lax.axis_size("tm") - 1).bit_length())
    cuts = cuts_of(5 * channels)
    in_keep_a, in_send_a, g1_b, pre0_b, now_b = run(
        third_body,
        ids,
        [local_b, from_next_b, slope_b, now_a, taps, wo],
        [(half, BF)] * 2 + third_outs,
        after=[keep1],
    )
    sums1 = split_sums(ids, keep1, swapped(send1), after=[now_b])
    keep0, send0 = weights(
        [x_a, x_h, pre0_a, hid0_a, g1_a, x_b, x_a, pre0_b, hid0_b, g1_b], after=sums1
    )
    sums0 = split_sums(ids, keep0, swapped(send0))
    sums1 = summed(ids, cuts, 0, sums1, sums0)
    in_keep_b, in_send_b = run(functools.partial(last_body, size), ids, [now_b, ahead_b], [(half, BF)] * 2, after=sums1)
    sums0 = summed(ids, cuts, 0, sums0, [in_keep_b])
    for step in range(1, steps):
        sums1 = summed(ids, cuts, step, sums1, sums0)
        sums0 = summed(ids, cuts, step, sums0, sums1)
    (output,) = run(
        assemble_body,
        ids,
        [out_keep_a, swapped(out_send_a), out_keep_b, swapped(out_send_b)],
        [((rows, half_width), BF)],
        after=[in_keep_b],
    )
    conv_grad, out_grad = placed_sums(ids, channels, cuts, sums0, sums1)
    (in_grad,) = run(
        assemble_body,
        ids,
        [in_keep_a, swapped(in_send_a), in_keep_b, swapped(in_send_b)],
        [((rows, half_width), BF)],
    )
    return (
        output,
        in_grad,
        conv_grad.reshape(2, 2, channels, 2, half_width),
        out_grad.reshape(2, channels, half_width),
    )


def solution(mesh):
    placed = (P(("groups", "tm"), "chan"), P(("groups", "tm"), "chan"), P(), P())
    return jax.shard_map(
        on_device,
        mesh=mesh,
        in_specs=placed,
        out_specs=(
            P(("groups", "tm"), "chan"),
            P(("groups", "tm"), "chan"),
            P("groups", None, None, None, "chan"),
            P("groups", None, "chan"),
        ),
        check_vma=False,
    )
```

```python
import functools
import math

import jax
import jax.numpy as jnp
from jax import lax
from jax.experimental import pallas as pl
from jax.experimental.pallas import tpu as pltpu
from jax.sharding import PartitionSpec as P

BF = jnp.bfloat16
F32 = jnp.float32
VMEM_LIMIT = 24 * 1024 * 1024
CHUNK = 256


def mm(a, b):
    return jnp.dot(a, b, preferred_element_type=F32)


def mm_t(a, b):
    return lax.dot_general(a, b, (((1,), (1,)), ((), ())), preferred_element_type=F32)


def mm_rows(a, b):
    return lax.dot_general(a, b, (((0,), (0,)), ((), ())), preferred_element_type=F32)


def ordered(core, own, other):
    first = core == 0
    return jnp.concatenate(
        [jnp.where(first, own, other), jnp.where(first, other, own)], axis=1
    )


def halves(core, values):
    width = values.shape[1] // 2
    low, high = values[:, :width], values[:, width:]
    first = core == 0
    return jnp.where(first, low, high), jnp.where(first, high, low)


def chunks(ref):
    return [pl.ds(r, CHUNK) for r in range(0, ref.shape[0], CHUNK)]


class Place:
    def __getitem__(self, axis):
        return lax.axis_index(("chan", "tm")[axis])


def run(body, ids, ins, outs, scratch=(), after=()):
    count = len(ins)

    def kernel(*refs):
        body(ids, *refs[:count], *refs[count + len(after) :])

    return pl.pallas_call(
        kernel,
        in_specs=[pl.BlockSpec(memory_space=pltpu.VMEM)] * count
        + [pl.BlockSpec(memory_space=pl.ANY)] * len(after),
        out_specs=[pl.BlockSpec(memory_space=pltpu.VMEM)] * len(outs),
        out_shape=[jax.ShapeDtypeStruct(shape, kind) for shape, kind in outs],
        scratch_shapes=list(scratch),
        compiler_params=pltpu.CompilerParams(vmem_limit_bytes=VMEM_LIMIT),
        cost_estimate=pl.CostEstimate(flops=1, bytes_accessed=1, transcendentals=0),
    )(*ins, *after)


def gated(x, delayed, taps, layer):
    width = x.shape[1]
    preact = mm(x, taps[layer, 0]) + mm(delayed, taps[layer, 1])
    filt = jnp.tanh(preact[:, :width])
    gate = 0.5 * jnp.tanh(0.5 * preact[:, width:]) + 0.5
    hidden = (filt * gate).astype(BF)
    return hidden, gate * (1.0 - filt * filt), filt * gate * (1.0 - gate)


def gather_body(ids, own, other, a_o, b_o):
    core = ids[0]
    count = a_o.shape[0]
    for half, out in ((0, a_o), (1, b_o)):
        for rows in chunks(out):
            place = pl.ds(pl.multiple_of((half * 2 + core) * count + rows.start, CHUNK), CHUNK)
            out[rows, :] = ordered(core, own[place, :], other[place, :])


def cot_body(ids, own, other, wo, a_o, b_o, ha_o, hb_o):
    gather_body(ids, own, other, a_o, b_o)
    for g_r, h_r in ((a_o, ha_o), (b_o, hb_o)):
        for rows in chunks(g_r):
            h_r[rows, :] = mm_t(g_r[rows, :], wo[1])


def first_body(ids, x_r, d_r, taps, wo, x1_o, hid_o, slope_o):
    width = x_r.shape[1]
    for rows in chunks(x_r):
        x = x_r[rows, :]
        hidden, sf, sg = gated(x, d_r[rows, :], taps, 0)
        hid_o[rows, :] = hidden
        slope_o[rows, :width] = sf
        slope_o[rows, width:] = sg
        x1_o[rows, :] = (x.astype(F32) + mm(hidden, wo[0])).astype(BF)


def pre_grad(hg, sf, sg):
    return jnp.concatenate([(hg * sf).astype(BF), (hg * sg).astype(BF)], axis=1)


def second_body(ids, x_r, d_r, hg_r, taps, pre_o, past_o, hid_o):
    for rows in chunks(x_r):
        hidden, sf, sg = gated(x_r[rows, :], d_r[rows, :], taps, 1)
        hid_o[rows, :] = hidden
        pre = pre_grad(hg_r[rows, :], sf, sg)
        pre_o[rows, :] = pre
        past_o[rows, :] = mm_t(pre, taps[1, 1]).astype(BF)


def rest_body(ids, x_r, hid_r, g_r, pre_r, taps, wo, keep_o, send_o, local_o):
    for rows in chunks(x_r):
        out = (x_r[rows, :].astype(F32) + mm(hid_r[rows, :], wo[1])).astype(BF)
        keep, send = halves(ids[0], out)
        keep_o[rows, :] = keep
        send_o[rows, :] = send
        local_o[rows, :] = g_r[rows, :].astype(F32) + mm_t(pre_r[rows, :], taps[1, 0])


def later_body(ids, x_r, d_r, g_r, taps, wo, term_o):
    for rows in chunks(d_r):
        _, sf, sg = gated(x_r[rows, :], d_r[rows, :], taps, 1)
        pre = pre_grad(mm_t(g_r[rows, :], wo[1]), sf, sg)
        term_o[rows, :] = mm_t(pre, taps[1, 1])


def third_rows(rows, g, slope_r, taps, wo, g_o, pre_o, now_o):
    width = g.shape[1]
    g_o[rows, :] = g
    pre = pre_grad(mm_t(g, wo[0]), slope_r[rows, :width], slope_r[rows, width:])
    pre_o[rows, :] = pre
    now_o[rows, :] = g.astype(F32) + mm_t(pre, taps[0, 0])
    return pre


def third_body(ids, local_r, arrived_r, slope_r, now_a, taps, wo, keep_o, send_o, *outs):
    for rows in chunks(local_r):
        g = (local_r[rows, :] + arrived_r[rows, :].astype(F32)).astype(BF)
        pre = third_rows(rows, g, slope_r, taps, wo, *outs)
        keep, send = halves(ids[0], (now_a[rows, :] + mm_t(pre, taps[0, 1])).astype(BF))
        keep_o[rows, :] = keep
        send_o[rows, :] = send


def both_body(ids, x_r, d_r, g_r, hg_r, term_r, slope_r, taps, wo, *outs):
    past_o, pre1_o, hid_o, keep_o, send_o = outs[:5]
    for rows in chunks(x_r):
        x = x_r[rows, :]
        hidden, sf, sg = gated(x, d_r[rows, :], taps, 1)
        hid_o[rows, :] = hidden
        pre = pre_grad(hg_r[rows, :], sf, sg)
        pre1_o[rows, :] = pre
        local = g_r[rows, :].astype(F32) + mm_t(pre, taps[1, 0])
        g = (local + term_r[rows, :]).astype(BF)
        pre = third_rows(rows, g, slope_r, taps, wo, *outs[5:])
        past_o[rows, :] = mm_t(pre, taps[0, 1]).astype(BF)
        out = (x.astype(F32) + mm(hidden, wo[1])).astype(BF)
        keep, send = halves(ids[0], out)
        keep_o[rows, :] = keep
        send_o[rows, :] = send


def last_body(size, ids, now_r, past_r, keep_o, send_o):
    ended = ids[1] == size - 1
    for rows in chunks(now_r):
        past = past_r[rows, :].astype(F32)
        past = jnp.where(ended, jnp.zeros_like(past), past)
        keep, send = halves(ids[0], (now_r[rows, :] + past).astype(BF))
        keep_o[rows, :] = keep
        send_o[rows, :] = send


def assemble_body(ids, keep_a, got_a, keep_b, got_b, out):
    core = ids[0]
    count = keep_a.shape[0]
    for half, keep, got in ((0, keep_a, got_a), (1, keep_b, got_b)):
        own = pl.multiple_of((half * 2 + core) * count, count)
        other = pl.multiple_of((half * 2 + 1 - core) * count, count)
        out[pl.ds(own, count), :] = keep[...]
        out[pl.ds(other, count), :] = got[...]


def weight_body(scale, ids, xa, da, pa, ha, ga, xb, db, pb, hb, gb, keep_o, send_o):
    channels = ha.shape[1]
    pairs = (
        (xa, pa, xb, pb),
        (da, pa, db, pb),
        (ha, ga, hb, gb),
    )
    position = 0
    for la, ra, lb, rb in pairs:
        both = (mm_rows(la[...], ra[...]) + mm_rows(lb[...], rb[...])) * scale
        for k in range(both.shape[1] // channels):
            keep, send = halves(ids[0], both[:, k * channels : (k + 1) * channels])
            keep_o[pl.ds(position * channels, channels), :] = keep
            send_o[pl.ds(position * channels, channels), :] = send.astype(BF)
            position += 1


def gather_sums(keep, got, total):
    channels = total.shape[0] // 5
    for position in range(5):
        rows = pl.ds(position * channels, channels)
        value = keep[rows, :] + got[rows, :].astype(F32)
        if position < 4:
            tap, k = divmod(position, 2)
            total[pl.ds(tap * 2 * channels + k, channels, stride=2), :] = value
        else:
            total[rows, :] = value


def side(ids, step):
    return (ids[1] // (1 << step)) % 2


def parted(ids, step, values, own_o, send_o):
    count = own_o.shape[0]
    own = side(ids, step)
    own_o[...] = values(pl.ds(pl.multiple_of(own * count, count), count))
    send_o[...] = values(pl.ds(pl.multiple_of((1 - own) * count, count), count)).astype(BF)


def split_body(ids, keep, got, own_o, send_o, total):
    gather_sums(keep, got, total)
    parted(ids, 0, lambda rows: total[rows, :], own_o, send_o)


def part_body(step, ids, own, got, own_o, send_o):
    parted(
        ids, step, lambda rows: own[rows, :] + got[rows, :].astype(F32), own_o, send_o
    )


def add_body(ids, own, got, total_o):
    total_o[...] = (own[...].astype(F32) + got[...].astype(F32)).astype(BF)


def join_body(ids, first, second, both_o):
    rows = first.shape[0]
    both_o[:rows, :] = first[...]
    both_o[rows:, :] = second[...]


def place_body(cuts, first, ids, *refs):
    conv_o, out_o = refs[-2:]
    pieces = 1 << cuts
    rows = refs[0].shape[0]
    layers = (refs[:first], refs[first:-2])
    conv_rows = conv_o.shape[0] // 2
    out_rows = out_o.shape[0] // 2
    for layer in (0, 1):
        held = []
        for ref in layers[layer]:
            held += [ref[r : r + rows, :] for r in range(0, ref.shape[0], rows)]
        for bit in range(cuts):
            swap = side(ids, cuts - 1 - bit) == 1
            held = [
                jnp.where(swap, held[i ^ (1 << bit)], held[i]) for i in range(pieces)
            ]
        for i in range(pieces):
            value = held[i].astype(F32)
            start = i * rows
            for k in range(0, rows, 64):
                at = start + k
                if at < conv_rows:
                    conv_o[layer * conv_rows + at : layer * conv_rows + at + 64, :] = value[k : k + 64]
                else:
                    at += layer * out_rows - conv_rows
                    out_o[at : at + 64, :] = value[k : k + 64]


def plain_body(ids, keep, got, total):
    gather_sums(keep, got, total)


def moved_by(values, distance):
    devices = range(lax.axis_size("tm"))
    return lax.ppermute(
        values, "tm", [(i, i + distance) for i in devices if i + distance in devices]
    )


def crossed(values, bit):
    return lax.ppermute(values, "tm", [(i, i ^ bit) for i in range(lax.axis_size("tm"))])


def swapped(values):
    return lax.ppermute(values, "chan", [(0, 1), (1, 0)])


def cuts_of(rows):
    size = lax.axis_size("tm")
    if size < 2 or size & (size - 1) or rows % 64:
        return 0
    return min(2, size.bit_length() - 1)


def split_sums(ids, keep, got, after=()):
    rows, cols = keep.shape
    if not cuts_of(rows):
        return run(plain_body, ids, [keep, got], [((rows, cols), F32)], after=after)
    return run(
        split_body,
        ids,
        [keep, got],
        [((rows // 2, cols), F32), ((rows // 2, cols), BF)],
        [pltpu.VMEM((rows, cols), F32)],
        after=after,
    )


def summed(ids, cuts, step, parts, after):
    if not cuts:
        return parts
    if step < cuts:
        own, send = parts
    else:
        own = send = parts[0]
    got = crossed(send, 1 << step)
    rows, cols = own.shape
    if step + 1 < cuts:
        return run(
            functools.partial(part_body, step + 1),
            ids,
            [own, got],
            [((rows // 2, cols), F32), ((rows // 2, cols), BF)],
            after=after,
        )
    return run(add_body, ids, [own, got], [(own.shape, BF)], after=after)


def spread(ids, cuts, total, after):
    held = [total]
    for step in reversed(range(cuts)):
        both = held[0]
        if len(held) > 1:
            rows, cols = both.shape
            (both,) = run(join_body, ids, held, [((2 * rows, cols), BF)], after=after)
        held.append(crossed(both, 1 << step))
    return held


def placed_sums(ids, channels, cuts, sums0, sums1):
    if not cuts:
        both = jnp.stack([lax.psum(sums[0], "tm") for sums in (sums0, sums1)])
        return both[:, : 4 * channels], both[:, 4 * channels :]
    cols = sums0[0].shape[1]
    late = spread(ids, cuts, sums1[0], [sums0[0]])
    own = sums0[0]
    soon = [own] + [crossed(own, partner) for partner in ((2, 1, 3) if cuts == 2 else (1,))]
    return run(
        functools.partial(place_body, cuts, len(soon)),
        ids,
        soon + late,
        [((8 * channels, cols), F32), ((2 * channels, cols), F32)],
    )


def on_device(signal, cotangent, conv_weight, out_weight):
    rows, half_width = signal.shape
    channels = conv_weight.shape[2]
    quarter = rows // 4
    wide = 2 * channels
    scale = 1.0 / math.sqrt(rows * lax.axis_size("tm"))
    later = 2
    ids = Place()
    taps = conv_weight.reshape(2, 2, channels, wide)
    wo = out_weight

    narrow, broad = (quarter, channels), (quarter, wide)
    half = (quarter, half_width)
    third_outs = [(narrow, BF), (broad, BF), (narrow, F32)]

    x_a, x_b = run(
        gather_body, ids, [signal, swapped(signal)], [(narrow, BF)] * 2, after=[taps]
    )
    x_h = moved_by(x_b, 1)
    first_outs = [(narrow, BF)] * 2 + [(broad, F32)]
    cot_a, cot_b, hg_a, hg_b = run(
        cot_body,
        ids,
        [cotangent, swapped(cotangent), wo],
        [(narrow, BF)] * 2 + [(narrow, F32)] * 2,
        after=[x_b],
    )
    cot_a_later = moved_by(cot_a, -later)
    x1_b, hid0_b, slope_b = run(
        first_body, ids, [x_b, x_a, taps, wo], first_outs, after=[cot_a]
    )
    x1_b_past = moved_by(x1_b, later)
    x1_a, hid0_a, slope_a = run(
        first_body, ids, [x_a, x_h, taps, wo], first_outs, after=[x1_b]
    )
    x1_a_later = moved_by(x1_a, -later)
    x1_a_past = moved_by(x1_a, later)

    pre1_b, to_past_b, hid1_b = run(
        second_body,
        ids,
        [x1_b, x1_b_past, hg_b, taps],
        [(broad, BF)] + [(narrow, BF)] * 2,
        after=[x1_a, cot_a_later],
    )
    from_next_b = moved_by(to_past_b, -later)
    out_keep_b, out_send_b, local_b = run(
        rest_body,
        ids,
        [x1_b, hid1_b, cot_b, pre1_b, taps, wo],
        [(half, BF)] * 2 + [(narrow, F32)],
    )
    (term_a,) = run(
        later_body,
        ids,
        [x1_a_later, x1_a, cot_a_later, taps, wo],
        [(narrow, F32)],
        after=[local_b],
    )
    past_a, pre1_a, hid1_a, out_keep_a, out_send_a, g1_a, pre0_a, now_a = run(
        both_body,
        ids,
        [x1_a, x1_a_past, cot_a, hg_a, term_a, slope_a, taps, wo],
        [(narrow, BF), (broad, BF), (narrow, BF), (half, BF), (half, BF)] + third_outs,
    )
    size = lax.axis_size("tm")
    ahead_b = moved_by(past_a, -1)

    def weights(arrays, after=()):
        shape = (5 * channels, half_width)
        return run(
            functools.partial(weight_body, scale),
            ids,
            arrays,
            [(shape, F32), (shape, BF)],
            after=after,
        )

    keep1, send1 = weights(
        [x1_a, x1_a_past, pre1_a, hid1_a, cot_a, x1_b, x1_b_past, pre1_b, hid1_b, cot_b]
    )
    steps = max(1, (lax.axis_size("tm") - 1).bit_length())
    cuts = cuts_of(5 * channels)
    in_keep_a, in_send_a, g1_b, pre0_b, now_b = run(
        third_body,
        ids,
        [local_b, from_next_b, slope_b, now_a, taps, wo],
        [(half, BF)] * 2 + third_outs,
        after=[keep1],
    )
    sums1 = split_sums(ids, keep1, swapped(send1), after=[now_b])
    keep0, send0 = weights(
        [x_a, x_h, pre0_a, hid0_a, g1_a, x_b, x_a, pre0_b, hid0_b, g1_b], after=sums1
    )
    sums0 = split_sums(ids, keep0, swapped(send0))
    sums1 = summed(ids, cuts, 0, sums1, sums0)
    in_keep_b, in_send_b = run(functools.partial(last_body, size), ids, [now_b, ahead_b], [(half, BF)] * 2, after=sums1)
    sums0 = summed(ids, cuts, 0, sums0, [in_keep_b])
    for step in range(1, steps):
        sums1 = summed(ids, cuts, step, sums1, sums0)
        sums0 = summed(ids, cuts, step, sums0, sums1)
    (output,) = run(
        assemble_body,
        ids,
        [out_keep_a, swapped(out_send_a), out_keep_b, swapped(out_send_b)],
        [((rows, half_width), BF)],
        after=[in_keep_b],
    )
    conv_grad, out_grad = placed_sums(ids, channels, cuts, sums0, sums1)
    (in_grad,) = run(
        assemble_body,
        ids,
        [in_keep_a, swapped(in_send_a), in_keep_b, swapped(in_send_b)],
        [((rows, half_width), BF)],
    )
    return (
        output,
        in_grad,
        conv_grad.reshape(2, 2, channels, 2, half_width),
        out_grad.reshape(2, channels, half_width),
    )


def solution(mesh):
    placed = (P(("groups", "tm"), "chan"), P(("groups", "tm"), "chan"), P(), P())
    return jax.shard_map(
        on_device,
        mesh=mesh,
        in_specs=placed,
        out_specs=(
            P(("groups", "tm"), "chan"),
            P(("groups", "tm"), "chan"),
            P("groups", None, None, None, "chan"),
            P("groups", None, "chan"),
        ),
        check_vma=False,
    )
```

```python
import functools
import math

import jax
import jax.numpy as jnp
from jax import lax
from jax.experimental import pallas as pl
from jax.experimental.pallas import tpu as pltpu
from jax.sharding import PartitionSpec as P

BF = jnp.bfloat16
F32 = jnp.float32
VMEM_LIMIT = 24 * 1024 * 1024
CHUNK = 256


def mm(a, b):
    return jnp.dot(a, b, preferred_element_type=F32)


def mm_t(a, b):
    return lax.dot_general(a, b, (((1,), (1,)), ((), ())), preferred_element_type=F32)


def mm_rows(a, b):
    return lax.dot_general(a, b, (((0,), (0,)), ((), ())), preferred_element_type=F32)


def ordered(core, own, other):
    first = core == 0
    return jnp.concatenate(
        [jnp.where(first, own, other), jnp.where(first, other, own)], axis=1
    )


def halves(core, values):
    width = values.shape[1] // 2
    low, high = values[:, :width], values[:, width:]
    first = core == 0
    return jnp.where(first, low, high), jnp.where(first, high, low)


def chunks(ref):
    return [pl.ds(r, CHUNK) for r in range(0, ref.shape[0], CHUNK)]


class Place:
    def __getitem__(self, axis):
        return lax.axis_index(("chan", "tm")[axis])


def run(body, ids, ins, outs, scratch=(), after=()):
    count = len(ins)

    def kernel(*refs):
        body(ids, *refs[:count], *refs[count + len(after) :])

    return pl.pallas_call(
        kernel,
        in_specs=[pl.BlockSpec(memory_space=pltpu.VMEM)] * count
        + [pl.BlockSpec(memory_space=pl.ANY)] * len(after),
        out_specs=[pl.BlockSpec(memory_space=pltpu.VMEM)] * len(outs),
        out_shape=[jax.ShapeDtypeStruct(shape, kind) for shape, kind in outs],
        scratch_shapes=list(scratch),
        compiler_params=pltpu.CompilerParams(vmem_limit_bytes=VMEM_LIMIT),
        cost_estimate=pl.CostEstimate(flops=1, bytes_accessed=1, transcendentals=0),
    )(*ins, *after)


def gated(x, delayed, taps, layer):
    width = x.shape[1]
    preact = mm(x, taps[layer, 0]) + mm(delayed, taps[layer, 1])
    filt = jnp.tanh(preact[:, :width])
    gate = 0.5 * jnp.tanh(0.5 * preact[:, width:]) + 0.5
    hidden = (filt * gate).astype(BF)
    return hidden, gate * (1.0 - filt * filt), filt * gate * (1.0 - gate)


def gather_body(ids, own, other, a_o, b_o):
    core = ids[0]
    count = a_o.shape[0]
    for half, out in ((0, a_o), (1, b_o)):
        for rows in chunks(out):
            place = pl.ds(pl.multiple_of((half * 2 + core) * count + rows.start, CHUNK), CHUNK)
            out[rows, :] = ordered(core, own[place, :], other[place, :])


def cot_body(ids, own, other, wo, a_o, b_o, ha_o, hb_o):
    gather_body(ids, own, other, a_o, b_o)
    for g_r, h_r in ((a_o, ha_o), (b_o, hb_o)):
        for rows in chunks(g_r):
            h_r[rows, :] = mm_t(g_r[rows, :], wo[1])


def first_body(ids, x_r, d_r, taps, wo, x1_o, hid_o, slope_o):
    width = x_r.shape[1]
    for rows in chunks(x_r):
        x = x_r[rows, :]
        hidden, sf, sg = gated(x, d_r[rows, :], taps, 0)
        hid_o[rows, :] = hidden
        slope_o[rows, :width] = sf
        slope_o[rows, width:] = sg
        x1_o[rows, :] = (x.astype(F32) + mm(hidden, wo[0])).astype(BF)


def pre_grad(hg, sf, sg):
    return jnp.concatenate([(hg * sf).astype(BF), (hg * sg).astype(BF)], axis=1)


def second_body(ids, x_r, d_r, hg_r, taps, pre_o, past_o, hid_o):
    for rows in chunks(x_r):
        hidden, sf, sg = gated(x_r[rows, :], d_r[rows, :], taps, 1)
        hid_o[rows, :] = hidden
        pre = pre_grad(hg_r[rows, :], sf, sg)
        pre_o[rows, :] = pre
        past_o[rows, :] = mm_t(pre, taps[1, 1]).astype(BF)


def rest_body(ids, x_r, hid_r, g_r, pre_r, taps, wo, keep_o, send_o, local_o):
    for rows in chunks(x_r):
        out = (x_r[rows, :].astype(F32) + mm(hid_r[rows, :], wo[1])).astype(BF)
        keep, send = halves(ids[0], out)
        keep_o[rows, :] = keep
        send_o[rows, :] = send
        local_o[rows, :] = g_r[rows, :].astype(F32) + mm_t(pre_r[rows, :], taps[1, 0])


def later_body(ids, x_r, d_r, g_r, taps, wo, term_o):
    for rows in chunks(d_r):
        _, sf, sg = gated(x_r[rows, :], d_r[rows, :], taps, 1)
        pre = pre_grad(mm_t(g_r[rows, :], wo[1]), sf, sg)
        term_o[rows, :] = mm_t(pre, taps[1, 1])


def third_rows(rows, g, slope_r, taps, wo, g_o, pre_o, now_o):
    width = g.shape[1]
    g_o[rows, :] = g
    pre = pre_grad(mm_t(g, wo[0]), slope_r[rows, :width], slope_r[rows, width:])
    pre_o[rows, :] = pre
    now_o[rows, :] = g.astype(F32) + mm_t(pre, taps[0, 0])
    return pre


def third_body(ids, local_r, arrived_r, slope_r, now_a, taps, wo, keep_o, send_o, *outs):
    for rows in chunks(local_r):
        g = (local_r[rows, :] + arrived_r[rows, :].astype(F32)).astype(BF)
        pre = third_rows(rows, g, slope_r, taps, wo, *outs)
        keep, send = halves(ids[0], (now_a[rows, :] + mm_t(pre, taps[0, 1])).astype(BF))
        keep_o[rows, :] = keep
        send_o[rows, :] = send


def both_body(ids, x_r, d_r, g_r, hg_r, term_r, slope_r, taps, wo, *outs):
    past_o, pre1_o, hid_o, keep_o, send_o = outs[:5]
    for rows in chunks(x_r):
        x = x_r[rows, :]
        hidden, sf, sg = gated(x, d_r[rows, :], taps, 1)
        hid_o[rows, :] = hidden
        pre = pre_grad(hg_r[rows, :], sf, sg)
        pre1_o[rows, :] = pre
        local = g_r[rows, :].astype(F32) + mm_t(pre, taps[1, 0])
        g = (local + term_r[rows, :]).astype(BF)
        pre = third_rows(rows, g, slope_r, taps, wo, *outs[5:])
        past_o[rows, :] = mm_t(pre, taps[0, 1]).astype(BF)
        out = (x.astype(F32) + mm(hidden, wo[1])).astype(BF)
        keep, send = halves(ids[0], out)
        keep_o[rows, :] = keep
        send_o[rows, :] = send


def last_body(size, ids, now_r, past_r, keep_o, send_o):
    ended = ids[1] == size - 1
    for rows in chunks(now_r):
        past = past_r[rows, :].astype(F32)
        past = jnp.where(ended, jnp.zeros_like(past), past)
        keep, send = halves(ids[0], (now_r[rows, :] + past).astype(BF))
        keep_o[rows, :] = keep
        send_o[rows, :] = send


def assemble_body(ids, keep_a, got_a, keep_b, got_b, out):
    core = ids[0]
    count = keep_a.shape[0]
    for half, keep, got in ((0, keep_a, got_a), (1, keep_b, got_b)):
        own = pl.multiple_of((half * 2 + core) * count, count)
        other = pl.multiple_of((half * 2 + 1 - core) * count, count)
        out[pl.ds(own, count), :] = keep[...]
        out[pl.ds(other, count), :] = got[...]


def weight_body(scale, ids, xa, da, pa, ha, ga, xb, db, pb, hb, gb, keep_o, send_o):
    channels = ha.shape[1]
    pairs = (
        (xa, pa, xb, pb),
        (da, pa, db, pb),
        (ha, ga, hb, gb),
    )
    position = 0
    for la, ra, lb, rb in pairs:
        both = (mm_rows(la[...], ra[...]) + mm_rows(lb[...], rb[...])) * scale
        for k in range(both.shape[1] // channels):
            keep, send = halves(ids[0], both[:, k * channels : (k + 1) * channels])
            keep_o[pl.ds(position * channels, channels), :] = keep
            send_o[pl.ds(position * channels, channels), :] = send.astype(BF)
            position += 1


def gather_sums(keep, got, total):
    channels = total.shape[0] // 5
    for position in range(5):
        rows = pl.ds(position * channels, channels)
        value = keep[rows, :] + got[rows, :].astype(F32)
        if position < 4:
            tap, k = divmod(position, 2)
            total[pl.ds(tap * 2 * channels + k, channels, stride=2), :] = value
        else:
            total[rows, :] = value


def side(ids, step):
    return (ids[1] // (1 << step)) % 2


def parted(ids, step, values, own_o, send_o):
    count = own_o.shape[0]
    own = side(ids, step)
    own_o[...] = values(pl.ds(pl.multiple_of(own * count, count), count))
    send_o[...] = values(pl.ds(pl.multiple_of((1 - own) * count, count), count)).astype(BF)


def split_body(ids, keep, got, own_o, send_o, total):
    gather_sums(keep, got, total)
    parted(ids, 0, lambda rows: total[rows, :], own_o, send_o)


def part_body(step, ids, own, got, own_o, send_o):
    parted(
        ids, step, lambda rows: own[rows, :] + got[rows, :].astype(F32), own_o, send_o
    )


def add_body(ids, own, got, total_o):
    total_o[...] = (own[...].astype(F32) + got[...].astype(F32)).astype(BF)


def join_body(ids, first, second, both_o):
    rows = first.shape[0]
    both_o[:rows, :] = first[...]
    both_o[rows:, :] = second[...]


def place_body(cuts, first, ids, *refs):
    conv_o, out_o = refs[-2:]
    pieces = 1 << cuts
    rows = refs[0].shape[0]
    layers = (refs[:first], refs[first:-2])
    conv_rows = conv_o.shape[0] // 2
    out_rows = out_o.shape[0] // 2
    for layer in (0, 1):
        held = []
        for ref in layers[layer]:
            held += [ref[r : r + rows, :] for r in range(0, ref.shape[0], rows)]
        for bit in range(cuts):
            swap = side(ids, cuts - 1 - bit) == 1
            held = [
                jnp.where(swap, held[i ^ (1 << bit)], held[i]) for i in range(pieces)
            ]
        for i in range(pieces):
            value = held[i].astype(F32)
            start = i * rows
            for k in range(0, rows, 64):
                at = start + k
                if at < conv_rows:
                    conv_o[layer * conv_rows + at : layer * conv_rows + at + 64, :] = value[k : k + 64]
                else:
                    at += layer * out_rows - conv_rows
                    out_o[at : at + 64, :] = value[k : k + 64]


def plain_body(ids, keep, got, total):
    gather_sums(keep, got, total)


def moved_by(values, distance):
    devices = range(lax.axis_size("tm"))
    return lax.ppermute(
        values, "tm", [(i, i + distance) for i in devices if i + distance in devices]
    )


def crossed(values, bit):
    return lax.ppermute(values, "tm", [(i, i ^ bit) for i in range(lax.axis_size("tm"))])


def swapped(values):
    return lax.ppermute(values, "chan", [(0, 1), (1, 0)])


def cuts_of(rows):
    size = lax.axis_size("tm")
    if size < 2 or size & (size - 1) or rows % 64:
        return 0
    return min(2, size.bit_length() - 1)


def split_sums(ids, keep, got, after=()):
    rows, cols = keep.shape
    if not cuts_of(rows):
        return run(plain_body, ids, [keep, got], [((rows, cols), F32)], after=after)
    return run(
        split_body,
        ids,
        [keep, got],
        [((rows // 2, cols), F32), ((rows // 2, cols), BF)],
        [pltpu.VMEM((rows, cols), F32)],
        after=after,
    )


def summed(ids, cuts, step, parts, after):
    if not cuts:
        return parts
    if step < cuts:
        own, send = parts
    else:
        own = send = parts[0]
    got = crossed(send, 1 << step)
    rows, cols = own.shape
    if step + 1 < cuts:
        return run(
            functools.partial(part_body, step + 1),
            ids,
            [own, got],
            [((rows // 2, cols), F32), ((rows // 2, cols), BF)],
            after=after,
        )
    return run(add_body, ids, [own, got], [(own.shape, BF)], after=after)


def spread(ids, cuts, total, after):
    held = [total]
    for step in reversed(range(cuts)):
        both = held[0]
        if len(held) > 1:
            rows, cols = both.shape
            (both,) = run(join_body, ids, held, [((2 * rows, cols), BF)], after=after)
        held.append(crossed(both, 1 << step))
    return held


def placed_sums(ids, channels, cuts, sums0, sums1):
    if not cuts:
        both = jnp.stack([lax.psum(sums[0], "tm") for sums in (sums0, sums1)])
        return both[:, : 4 * channels], both[:, 4 * channels :]
    cols = sums0[0].shape[1]
    late = spread(ids, cuts, sums1[0], ())
    own = sums0[0]
    soon = [own] + [crossed(own, partner) for partner in ((2, 1, 3) if cuts == 2 else (1,))]
    return run(
        functools.partial(place_body, cuts, len(soon)),
        ids,
        soon + late,
        [((8 * channels, cols), F32), ((2 * channels, cols), F32)],
    )


def on_device(signal, cotangent, conv_weight, out_weight):
    rows, half_width = signal.shape
    channels = conv_weight.shape[2]
    quarter = rows // 4
    wide = 2 * channels
    scale = 1.0 / math.sqrt(rows * lax.axis_size("tm"))
    later = 2
    ids = Place()
    taps = conv_weight.reshape(2, 2, channels, wide)
    wo = out_weight

    narrow, broad = (quarter, channels), (quarter, wide)
    half = (quarter, half_width)
    third_outs = [(narrow, BF), (broad, BF), (narrow, F32)]

    x_a, x_b = run(
        gather_body, ids, [signal, swapped(signal)], [(narrow, BF)] * 2, after=[taps]
    )
    x_h = moved_by(x_b, 1)
    first_outs = [(narrow, BF)] * 2 + [(broad, F32)]
    cot_a, cot_b, hg_a, hg_b = run(
        cot_body,
        ids,
        [cotangent, swapped(cotangent), wo],
        [(narrow, BF)] * 2 + [(narrow, F32)] * 2,
        after=[x_b],
    )
    cot_a_later = moved_by(cot_a, -later)
    x1_b, hid0_b, slope_b = run(
        first_body, ids, [x_b, x_a, taps, wo], first_outs, after=[cot_a]
    )
    x1_b_past = moved_by(x1_b, later)
    x1_a, hid0_a, slope_a = run(
        first_body, ids, [x_a, x_h, taps, wo], first_outs, after=[x1_b]
    )
    x1_a_later = moved_by(x1_a, -later)
    x1_a_past = moved_by(x1_a, later)

    pre1_b, to_past_b, hid1_b = run(
        second_body,
        ids,
        [x1_b, x1_b_past, hg_b, taps],
        [(broad, BF)] + [(narrow, BF)] * 2,
        after=[x1_a, cot_a_later],
    )
    from_next_b = moved_by(to_past_b, -later)
    out_keep_b, out_send_b, local_b = run(
        rest_body,
        ids,
        [x1_b, hid1_b, cot_b, pre1_b, taps, wo],
        [(half, BF)] * 2 + [(narrow, F32)],
    )
    (term_a,) = run(
        later_body,
        ids,
        [x1_a_later, x1_a, cot_a_later, taps, wo],
        [(narrow, F32)],
        after=[local_b],
    )
    past_a, pre1_a, hid1_a, out_keep_a, out_send_a, g1_a, pre0_a, now_a = run(
        both_body,
        ids,
        [x1_a, x1_a_past, cot_a, hg_a, term_a, slope_a, taps, wo],
        [(narrow, BF), (broad, BF), (narrow, BF), (half, BF), (half, BF)] + third_outs,
    )
    size = lax.axis_size("tm")
    ahead_b = moved_by(past_a, -1)

    def weights(arrays, after=()):
        shape = (5 * channels, half_width)
        return run(
            functools.partial(weight_body, scale),
            ids,
            arrays,
            [(shape, F32), (shape, BF)],
            after=after,
        )

    keep1, send1 = weights(
        [x1_a, x1_a_past, pre1_a, hid1_a, cot_a, x1_b, x1_b_past, pre1_b, hid1_b, cot_b]
    )
    steps = max(1, (lax.axis_size("tm") - 1).bit_length())
    cuts = cuts_of(5 * channels)
    in_keep_a, in_send_a, g1_b, pre0_b, now_b = run(
        third_body,
        ids,
        [local_b, from_next_b, slope_b, now_a, taps, wo],
        [(half, BF)] * 2 + third_outs,
        after=[keep1],
    )
    sums1 = split_sums(ids, keep1, swapped(send1), after=[now_b])
    keep0, send0 = weights(
        [x_a, x_h, pre0_a, hid0_a, g1_a, x_b, x_a, pre0_b, hid0_b, g1_b], after=sums1
    )
    sums0 = split_sums(ids, keep0, swapped(send0))
    sums1 = summed(ids, cuts, 0, sums1, sums0)
    in_keep_b, in_send_b = run(functools.partial(last_body, size), ids, [now_b, ahead_b], [(half, BF)] * 2, after=sums1)
    sums0 = summed(ids, cuts, 0, sums0, [in_keep_b])
    for step in range(1, steps):
        sums1 = summed(ids, cuts, step, sums1, sums0)
        sums0 = summed(ids, cuts, step, sums0, sums1)
    (output,) = run(
        assemble_body,
        ids,
        [out_keep_a, swapped(out_send_a), out_keep_b, swapped(out_send_b)],
        [((rows, half_width), BF)],
        after=[in_keep_b],
    )
    conv_grad, out_grad = placed_sums(ids, channels, cuts, sums0, sums1)
    (in_grad,) = run(
        assemble_body,
        ids,
        [in_keep_a, swapped(in_send_a), in_keep_b, swapped(in_send_b)],
        [((rows, half_width), BF)],
    )
    return (
        output,
        in_grad,
        conv_grad.reshape(2, 2, channels, 2, half_width),
        out_grad.reshape(2, channels, half_width),
    )


def solution(mesh):
    placed = (P(("groups", "tm"), "chan"), P(("groups", "tm"), "chan"), P(), P())
    return jax.shard_map(
        on_device,
        mesh=mesh,
        in_specs=placed,
        out_specs=(
            P(("groups", "tm"), "chan"),
            P(("groups", "tm"), "chan"),
            P("groups", None, None, None, "chan"),
            P("groups", None, "chan"),
        ),
        check_vma=False,
    )
```
